32 devices in a mesh: members: 2 (over x), wave: 16 (over z, y, core).
Axes of the slice: x: 2, y: 2, z: 4, core: 2. Of those that a mesh axis runs over, the one named last changes fastest.
Arguments:
- grid_grad: bfloat16 [64, 640, 2560], P('members', 'wave'), parts along dimension 0, may hold values from -6 to 6
- legendre: bfloat16 [640, 1280, 320], P('wave'), may hold values from -0.25 to 0.25
- spectrum: float32 [1280], replicated, may hold values from 0.25 to 4
- owner_waves: int32 [640], replicated, may hold values from 0 to 639, each once
- lat_order: int32 [640], replicated, may hold values from 0 to 639, each once
Outputs:
- gradient_spectra: bfloat16 [1280, 64, 1280], P(('members', 'wave')), parts along dimension 0
- smoothed_grid: bfloat16 [64, 640, 2560], P('members', 'wave'), parts along dimension 0
The draws below stay inside these ranges and needn't reach their ends.
There are 2 independent parts, one for each index of `members`. The reference program is written for one: setup_inputs(seed, part) draws one part's arguments, and reference() takes and returns one part's arrays. A program takes and returns all parts, laid end to end along the dimension named above; an argument that names none is the same for every part. Nothing has to cross between parts.
Inputs may be any that keep to these rules, and one draw needn't show every extreme that they name: `owner_waves`: each zonal wavenumber is held by exactly one slot; a device along wave holds 640 / 16 consecutive slots. `lat_order`: each latitude is held by exactly one stored row; latitude j < 320 is northern row j and latitude 320 + j is its southern mirror.
All inputs are finite; a program needn't handle non-finite values.
Results may differ from the reference program's by a relative error of at most 0.015.
Values may be sent and summed in bfloat16 or wider, within the bound.
A program may use at most 256 MiB of HBM per device.

```python
import math
import jax
import jax.numpy as jnp
from jax import lax

NLON = 2560
NLAT = 640
NH = 320
MW = 640
NMAX = 1280
K = 32


def steps_of(rng, dims, shards, low, top_value):
    def one(position, blocks):
        steps = jax.random.uniform(jax.random.fold_in(jax.random.fold_in(rng, 6), position), (blocks,), jnp.float32, low / len(shards), top_value / len(shards))
        return jnp.repeat(jnp.exp(steps), dims[position] // blocks).reshape((-1,) + (1,) * (len(dims) - position - 1))

    gain = one(*shards[0])
    for cut in shards[1:]:
        gain = gain * one(*cut)
    return gain


def centred(stream_key, extent, scale, bound, pieces=(), kind=jnp.bfloat16):
    result = scale * jax.random.normal(stream_key, extent, jnp.float32)
    if pieces:
        result = result * steps_of(stream_key, extent, pieces, -0.22, 0.18)
    return jnp.clip(result, -bound, bound).astype(kind)


def setup_inputs(seed: int = 0, part: int = 0) -> dict:
    key_list = jax.random.split(jax.random.key(seed), 6)
    part_keys = jax.random.split(jax.random.fold_in(key_list[5], part), 6)
    grid_grad = centred(part_keys[0], (K, NLAT, NLON), 1.0, 6.0, ((1, 16),))
    legendre = centred(key_list[1], (MW, NMAX, NH), (2 * NH) ** -0.5, 0.25, ((0, 16),))
    spectrum = jnp.clip(jnp.exp(jax.random.uniform(key_list[2], (NMAX,), jnp.float32, math.log(0.25), math.log(4.0))), 0.25, 4.0)
    owner_waves = jax.random.permutation(key_list[3], MW).astype(jnp.int32)
    lat_order = jax.random.permutation(key_list[4], NLAT).astype(jnp.int32)
    return dict(grid_grad=grid_grad, legendre=legendre, spectrum=spectrum, owner_waves=owner_waves, lat_order=lat_order)


def reference(grid_grad, legendre, spectrum, owner_waves, lat_order):
    values = grid_grad.astype(jnp.float32)
    spectra = jnp.fft.rfft(values, axis=-1)[..., :MW] / math.sqrt(NLON)
    fourier = jnp.stack([jnp.real(spectra), jnp.imag(spectra)], axis=1).astype(jnp.bfloat16)
    rows_of = jnp.zeros((NLAT,), jnp.int32).at[lat_order].set(jnp.arange(NLAT, dtype=jnp.int32))
    by_lat = fourier[:, :, rows_of, :]

    def one_slot(pair):
        table, wave = pair
        columns = lax.dynamic_index_in_dim(by_lat, wave, 3, keepdims=False).reshape(2 * K, NLAT)
        north = jnp.dot(table, columns[:, :NH].T, preferred_element_type=jnp.float32)
        south = jnp.dot(table, columns[:, NH:].T, preferred_element_type=jnp.float32)
        offsets = jnp.arange(NMAX, dtype=jnp.int32) - wave
        sign = (1 - 2 * (offsets % 2)).astype(jnp.float32)[:, None]
        spec = jnp.where((offsets >= 0)[:, None], north + sign * south, 0.0)
        filtered = (spec * spectrum[:, None]).astype(jnp.bfloat16)
        upper = jnp.dot(table.T, filtered, preferred_element_type=jnp.float32)
        lower = jnp.dot(table.T, filtered * sign.astype(jnp.bfloat16), preferred_element_type=jnp.float32)
        folded = jnp.concatenate([upper, lower], axis=0).astype(jnp.bfloat16)
        return (spec.T.astype(jnp.bfloat16), folded)
    spec_all, folded_all = lax.map(one_slot, (legendre, owner_waves))
    stored = folded_all[:, lat_order, :].astype(jnp.float32).reshape(MW, NLAT, K, 2)
    real_part = jnp.transpose(stored[..., 0], (2, 1, 0))
    imag_part = jnp.transpose(stored[..., 1], (2, 1, 0))
    real_full = jnp.zeros((K, NLAT, NLON), jnp.float32).at[:, :, owner_waves].set(real_part)
    imag_full = jnp.zeros((K, NLAT, NLON), jnp.float32).at[:, :, owner_waves].set(imag_part)
    full = lax.complex(real_full, imag_full)
    smoothed = jnp.real(jnp.fft.ifft(full, axis=-1)) * (NLON / math.sqrt(MW))
    return (spec_all, smoothed.astype(jnp.bfloat16))
```

```python
import functools
import math

import jax
import jax.numpy as jnp
from jax import lax
from jax.experimental import pallas as pl
from jax.experimental.pallas import tpu as pltpu
from jax.sharding import PartitionSpec as P

LANES = 128
PARTS = 2
VMEM = 56 * 2**20
F32 = jnp.float32
BF16 = jnp.bfloat16


def up(value, step):
    return -(-value // step) * step


def params(**extra):
    return pltpu.CompilerParams(vmem_limit_bytes=VMEM, **extra)


def angle_tables(waves, lon_cells):
    owners, slots = waves.shape
    quarter = lon_cells // 4
    rows = jnp.stack([waves, waves], axis=1).reshape(-1, 1)
    shift = jnp.broadcast_to(jnp.arange(2, dtype=jnp.int32)[None, :, None] * quarter, (owners, 2, slots))
    coarse = rows * (jnp.arange(LANES, dtype=jnp.int32) * LANES % lon_cells) + shift.reshape(-1, 1)
    fine = rows * jnp.arange(LANES, dtype=jnp.int32)
    ticks = jnp.concatenate([coarse, fine], axis=1) % lon_cells
    angle = ticks.astype(F32) * (2.0 * math.pi / lon_cells)
    return jnp.concatenate([jnp.cos(angle), jnp.sin(angle)], axis=1)


def forward_body(owners, rows_dev, group, piece, factor, x_ref, angles_ref, y_ref, table_ref):
    lon_cells = x_ref.shape[1]

    @pl.when(pl.program_id(0) == 0)
    def _():
        def rows_step(t, carry):
            rows = pl.ds(pl.multiple_of(t * 16, 16), 16)
            cos_lo = angles_ref[rows, LANES : 2 * LANES]
            sin_lo = angles_ref[rows, 3 * LANES : 4 * LANES]
            cos_hi = angles_ref[rows, 0:LANES]
            sin_hi = angles_ref[rows, 2 * LANES : 3 * LANES]
            for b in range(lon_cells // LANES):
                value = cos_hi[:, b : b + 1] * cos_lo - sin_hi[:, b : b + 1] * sin_lo
                table_ref[rows, b * LANES : (b + 1) * LANES] = value.astype(BF16)
            return carry

        lax.fori_loop(0, angles_ref.shape[0] // 16, rows_step, 0)

    y = lax.dot_general(
        x_ref[...], table_ref[...], (((1,), (1,)), ((), ())), preferred_element_type=F32
    )
    y = y * factor
    for w in range(owners):
        parts = [
            y[k * rows_dev : (k + 1) * rows_dev, w * piece : (w + 1) * piece] for k in range(group)
        ]
        y_ref[w] = jnp.concatenate(parts, axis=1).astype(BF16)


def forward(x, angles, owners, rows_dev, items):
    lon_cells = x.shape[1]
    columns = angles.shape[0]
    piece = columns // owners
    group = LANES // math.gcd(piece, LANES)
    body = functools.partial(
        forward_body, owners, rows_dev, group, piece, 1.0 / math.sqrt(lon_cells)
    )
    return pl.pallas_call(
        body,
        grid=(items // group,),
        in_specs=[
            pl.BlockSpec((group * rows_dev, lon_cells), lambda g: (g, 0)),
            pl.BlockSpec((columns, 4 * LANES), lambda g: (0, 0)),
        ],
        out_specs=[
            pl.BlockSpec((owners, rows_dev, group * piece), lambda g: (0, 0, g)),
            pl.BlockSpec((columns, lon_cells), lambda g: (0, 0)),
        ],
        out_shape=[
            jax.ShapeDtypeStruct((owners, rows_dev, items * piece), BF16),
            jax.ShapeDtypeStruct((columns, lon_cells), BF16),
        ],
        compiler_params=params(),
        cost_estimate=pl.CostEstimate(
            flops=2 * x.size * columns, bytes_accessed=2 * (x.size + columns * lon_cells), transcendentals=0
        ),
        name="forward_fourier",
    )(x, angles)


def legendre_body(first, chunk, north, wave_ref, recv_ref, place_ref, leg_ref, spectrum_ref, *rest):
    spec_ref, back_ref, side, fold = rest[-4:]
    step = pl.program_id(0)
    blocks = side.shape[0]
    half = blocks // 2
    rows = side.shape[1]
    total = leg_ref.shape[2]
    items = rows // chunk
    tile = 256

    @pl.when(step == 0)
    def _():
        def unpack(t, carry):
            cols = pl.ds(pl.multiple_of(t * tile, tile), tile)
            value = lax.dot_general(
                recv_ref[:, cols], place_ref[...], (((0,), (0,)), ((), ())), preferred_element_type=F32
            )
            for b in range(blocks):
                side[b, cols, :] = value[:, b * LANES : (b + 1) * LANES]
            return carry

        lax.fori_loop(0, rows // tile, unpack, 0)

    mine = pl.ds(step, items, stride=chunk)
    upper = jnp.concatenate([side[b, mine, :] for b in range(half)], axis=1)
    lower = jnp.concatenate([side[b, mine, :] for b in range(half, blocks)], axis=1)
    columns = jnp.concatenate([upper, lower], axis=0)[:, :north].astype(BF16)
    table = leg_ref[0]
    result = jnp.dot(columns, table, preferred_element_type=F32)
    offsets = lax.broadcasted_iota(jnp.int32, (1, total), 1) - wave_ref[first + step]
    sign = jnp.where(offsets % 2 == 0, 1.0, -1.0).astype(F32)
    valid = offsets >= 0
    spec = jnp.where(valid, result[:items] + sign * result[items:], 0.0)
    spec_ref[0] = spec.astype(BF16)
    filtered = (spec * spectrum_ref[...]).astype(BF16).astype(F32)
    second = jnp.concatenate([filtered, filtered * sign], axis=0).astype(BF16)
    folded = lax.dot_general(second, table, (((1,), (1,)), ((), ())), preferred_element_type=F32)
    folded = folded.astype(BF16).astype(F32)
    pad = jnp.zeros((folded.shape[0], half * LANES - north), F32)
    folded = jnp.concatenate([folded, pad], axis=1) if pad.shape[1] else folded
    for b in range(half):
        lanes = slice(b * LANES, (b + 1) * LANES)
        fold[b, mine, :] = folded[:items, lanes]
        fold[half + b, mine, :] = folded[items:, lanes]

    @pl.when(step == pl.num_programs(0) - 1)
    def _():
        def pack(t, carry):
            cols = pl.ds(pl.multiple_of(t * tile, tile), tile)
            value = jnp.concatenate([fold[b, cols, :] for b in range(blocks)], axis=1).astype(BF16)
            back_ref[:, cols] = lax.dot_general(
                place_ref[...], value, (((1,), (1,)), ((), ())), preferred_element_type=F32
            ).astype(BF16)
            return carry

        lax.fori_loop(0, rows // tile, pack, 0)


def legendre_step(first, chunk, mine, recv, place, table, spectrum, spec_before):
    slots, north, total = table.shape
    lat_rows, columns = recv.shape
    items = columns // chunk
    blocks = place.shape[1] // LANES
    whole = lambda shape: pl.BlockSpec(shape, lambda s: (0,) * len(shape))
    in_specs = [
        pl.BlockSpec(memory_space=pltpu.SMEM),
        whole(recv.shape),
        whole(place.shape),
        pl.BlockSpec((1, north, total), lambda s: (s + first, 0, 0)),
        whole(spectrum.shape),
    ]
    args = [mine, recv, place, table, spectrum]
    aliases = {}
    if spec_before is not None:
        in_specs.append(pl.BlockSpec(memory_space=pl.ANY))
        aliases = {len(args): 0}
        args.append(spec_before)
    return pl.pallas_call(
        functools.partial(legendre_body, first, chunk, north),
        grid=(chunk,),
        in_specs=in_specs,
        out_specs=[
            pl.BlockSpec((1, items, total), lambda s: (s + first, 0, 0)),
            whole(recv.shape),
        ],
        out_shape=[
            jax.ShapeDtypeStruct((slots, items, total), BF16),
            jax.ShapeDtypeStruct(recv.shape, BF16),
        ],
        scratch_shapes=[
            pltpu.VMEM((blocks, columns, LANES), F32),
            pltpu.VMEM((blocks, columns, LANES), F32),
        ],
        input_output_aliases=aliases,
        compiler_params=params(),
        cost_estimate=pl.CostEstimate(
            flops=8 * chunk * north * total * items,
            bytes_accessed=2 * chunk * total * (north + items),
            transcendentals=0,
        ),
        name="legendre_both_ways",
    )(*args)


def inverse_body(parts, rows_dev, group, piece, factor, *refs):
    returned, tables, out_ref = refs[:parts], refs[parts : 2 * parts], refs[-1]
    owners = returned[0].shape[0]
    total = None
    for ret_ref, table_ref in zip(returned, tables):
        blocks = [ret_ref[w].astype(F32) for w in range(owners)]
        rows = [
            jnp.concatenate([b[:, k * piece : (k + 1) * piece] for b in blocks], axis=1)
            for k in range(group)
        ]
        z = jnp.concatenate(rows, axis=0).astype(BF16)
        term = jnp.dot(z, table_ref[...], preferred_element_type=F32)
        total = term if total is None else total + term
    out_ref[...] = (total * factor).astype(BF16)


def inverse(returned, tables, waves_count):
    owners, rows_dev, lanes = returned[0].shape
    columns, lon_cells = tables[0].shape
    piece = columns // owners
    items = lanes // piece
    group = LANES // math.gcd(piece, LANES)
    body = functools.partial(
        inverse_body, len(tables), rows_dev, group, piece, 1.0 / math.sqrt(waves_count)
    )
    return pl.pallas_call(
        body,
        grid=(items // group,),
        in_specs=[pl.BlockSpec((owners, rows_dev, group * piece), lambda g: (0, 0, g))] * len(tables)
        + [pl.BlockSpec((columns, lon_cells), lambda g: (0, 0))] * len(tables),
        out_specs=pl.BlockSpec((group * rows_dev, lon_cells), lambda g: (g, 0)),
        out_shape=jax.ShapeDtypeStruct((items * rows_dev, lon_cells), BF16),
        compiler_params=params(),
        name="inverse_fourier",
    )(*returned, *tables)


def kernels_fit(items, rows_dev, slots, north, total, lon_cells):
    chunk = slots // PARTS
    piece = 2 * chunk
    group = LANES // math.gcd(piece, LANES)
    return (
        slots % PARTS == 0
        and rows_dev % 8 == 0
        and items % group == 0
        and 2 * items * chunk % 256 == 0
        and total % LANES == 0
        and lon_cells % (4 * LANES) == 0
        and piece % 8 == 0
    )


def local_kernels(grid_grad, legendre, spectrum, owner_waves, lat_order):
    owners = lax.axis_size("wave")
    items, rows_dev, lon_cells = grid_grad.shape
    slots, total, north = legendre.shape
    lat_rows = rows_dev * owners
    chunk = slots // PARTS
    waves = owner_waves.reshape(owners, slots)
    mine = lax.dynamic_index_in_dim(waves, lax.axis_index("wave"), 0, keepdims=False)
    x = grid_grad.reshape(items * rows_dev, lon_cells)
    table = jnp.swapaxes(legendre, 1, 2)
    half = up(north, LANES)
    column = jnp.where(lat_order < north, lat_order, lat_order - north + half)
    place = (column[:, None] == lax.iota(jnp.int32, 2 * half)[None, :]).astype(BF16)
    tables, received = [], []
    for h in range(PARTS):
        angles = angle_tables(waves[:, h * chunk : (h + 1) * chunk], lon_cells)
        sent, phases = forward(x, angles, owners, rows_dev, items)
        tables.append(phases)
        received.append(lax.all_to_all(sent, "wave", split_axis=0, concat_axis=0, tiled=True))
    spec = None
    returned = []
    for h in range(PARTS):
        recv = received[h].reshape(lat_rows, -1)
        spec, back = legendre_step(
            h * chunk, chunk, mine, recv, place, table, spectrum[None, :], spec
        )
        back = back.reshape(received[h].shape)
        returned.append(lax.all_to_all(back, "wave", split_axis=0, concat_axis=0, tiled=True))
    smoothed = inverse(returned, tables, owners * slots)
    return (spec, smoothed.reshape(grid_grad.shape))


def phase_table(waves, lon_cells, factor):
    ticks = lax.iota(jnp.int32, lon_cells)
    turns = waves[..., None] * ticks % lon_cells
    angle = turns.astype(jnp.float32) * (2.0 * math.pi / lon_cells)
    return jnp.stack([jnp.cos(angle), -jnp.sin(angle)], axis=1) * factor


def split_table(table):
    high_part = table.astype(jnp.bfloat16)
    low_part = (table - high_part.astype(jnp.float32)).astype(jnp.bfloat16)
    return (high_part, low_part)


def row_signs(count, wave):
    offsets = lax.iota(jnp.int32, count) - wave[..., None]
    return ((1 - 2 * (offsets % 2)).astype(jnp.float32), offsets >= 0)


def legendre_padded(legendre, side, spectrum, mine):
    half = side.shape[2] // 2
    result = jnp.einsum("snj,sjc->scn", legendre, side, preferred_element_type=jnp.float32)
    sign, valid = row_signs(legendre.shape[1], mine)
    spec = jnp.where(valid[:, None, :], result[:, :half] + sign[:, None, :] * result[:, half:], 0.0)
    filtered = (spec * spectrum).astype(jnp.bfloat16)
    second = jnp.concatenate([filtered, filtered * sign[:, None, :].astype(jnp.bfloat16)], axis=1)
    folded = jnp.einsum("snj,scn->scj", legendre, second, preferred_element_type=jnp.float32)
    return (spec, folded)


def local_plain(grid_grad, legendre, spectrum, owner_waves, lat_order):
    owners = lax.axis_size("wave")
    fields_levels, rows_dev, lon_cells = grid_grad.shape
    slots, total_rows, north_rows = legendre.shape
    lat_rows = rows_dev * owners
    waves = owner_waves.reshape(owners, slots)
    mine = lax.dynamic_index_in_dim(waves, lax.axis_index("wave"), 0, keepdims=False)
    forward_high, forward_low = split_table(
        phase_table(waves, lon_cells, 1.0 / math.sqrt(lon_cells))
    )
    inverse_high, inverse_low = split_table(
        phase_table(waves, lon_cells, 1.0 / math.sqrt(owners * slots))
    )
    onehot = (lat_order[None, :] == lax.iota(jnp.int32, lat_rows)[:, None]).astype(jnp.bfloat16)
    onehot = onehot.reshape(2, north_rows, owners, rows_dev)
    fourier = jnp.einsum(
        "kri,wpsi->wkrps", grid_grad, forward_high, preferred_element_type=jnp.float32
    )
    fourier = fourier + jnp.einsum(
        "kri,wpsi->wkrps", grid_grad, forward_low, preferred_element_type=jnp.float32
    )
    fourier = fourier.astype(jnp.bfloat16).reshape(owners, fields_levels, rows_dev, 2 * slots)
    received = lax.all_to_all(fourier, "wave", split_axis=0, concat_axis=0, tiled=True)
    items = received.shape[1]
    split = received.reshape(owners, items, rows_dev, 2, slots)
    side = jnp.einsum("hjwr,wkrps->sjhkp", onehot, split, preferred_element_type=jnp.float32)
    side = side.astype(jnp.bfloat16).reshape(slots, north_rows, 4 * items)
    spec, folded = legendre_padded(legendre, side, spectrum, mine)
    folded = folded.astype(jnp.bfloat16).reshape(slots, 2, items, 2, north_rows)
    back = jnp.einsum("hjwr,shkpj->wkrps", onehot, folded, preferred_element_type=jnp.float32)
    back = back.astype(jnp.bfloat16).reshape(owners, items, rows_dev, 2 * slots)
    returned = lax.all_to_all(back, "wave", split_axis=0, concat_axis=0, tiled=True)
    spec_out = spec.reshape(slots, items, 2, total_rows).astype(jnp.bfloat16)
    spec_out, returned = (spec_out, returned)
    gradient_spectra = spec_out.reshape(slots, 2 * fields_levels, total_rows)
    returned = returned.reshape(owners, fields_levels, rows_dev, 2, slots)
    smoothed = jnp.einsum(
        "wkrps,wpsi->kri", returned, inverse_high, preferred_element_type=jnp.float32
    )
    smoothed = smoothed + jnp.einsum(
        "wkrps,wpsi->kri", returned, inverse_low, preferred_element_type=jnp.float32
    )
    return (gradient_spectra, smoothed.astype(jnp.bfloat16))


def local(grid_grad, legendre, spectrum, owner_waves, lat_order):
    slots, total, north = legendre.shape
    if kernels_fit(*grid_grad.shape[:2], slots, north, total, grid_grad.shape[2]):
        return local_kernels(grid_grad, legendre, spectrum, owner_waves, lat_order)
    return local_plain(grid_grad, legendre, spectrum, owner_waves, lat_order)


def solution(mesh):
    in_specs = (P("members", "wave", None), P("wave", None, None), P(), P(), P())
    out_specs = (P(("members", "wave"), None, None), P("members", "wave", None))
    return jax.shard_map(local, mesh=mesh, in_specs=in_specs, out_specs=out_specs, check_vma=False)
```

```python
import functools
import math

import jax
import jax.numpy as jnp
from jax import lax
from jax.experimental import pallas as pl
from jax.experimental.pallas import tpu as pltpu
from jax.sharding import PartitionSpec as P

LANES = 128
PARTS = 4
VMEM = 56 * 2**20
F32 = jnp.float32
BF16 = jnp.bfloat16


def up(value, step):
    return -(-value // step) * step


def params(**extra):
    return pltpu.CompilerParams(vmem_limit_bytes=VMEM, **extra)


def angle_tables(waves, lon_cells):
    chunks, owners, slots = waves.shape
    quarter = lon_cells // 4
    coarse_count = lon_cells // LANES
    rows = jnp.broadcast_to(waves[:, :, None, :], (chunks, owners, 2, slots)).reshape(-1, 1)
    turn = jnp.arange(2, dtype=jnp.int32)[None, None, :, None] * quarter
    turn = jnp.broadcast_to(turn, (chunks, owners, 2, slots)).reshape(-1, 1)
    fine = rows * jnp.arange(LANES, dtype=jnp.int32)
    coarse = rows * (jnp.arange(coarse_count, dtype=jnp.int32) * LANES) + turn
    ticks = jnp.concatenate([fine, fine + 3 * quarter, coarse, coarse + 3 * quarter], axis=1) % lon_cells
    return jnp.cos(ticks.astype(F32) * (2.0 * math.pi / lon_cells))


def exchange_body(
    owners, chunks, wave_ref, x_hbm, angles_ref, place_ref, leg_hbm, spectrum_ref,
    spec_hbm, returned_hbm, table_hbm,
    x_ref, table_ref, y_ref, sent, recv, back, side, fold, leg_buf, spec_buf,
    fsend, frecv, bsend, brecv, load_sem, leg_sem, spec_sem, own_sem,
):
    slots, north, total = leg_hbm.shape
    lon_cells = x_hbm.shape[1]
    chunk = slots // chunks
    piece = 2 * chunk
    rows_dev = sent.shape[2]
    lanes = sent.shape[3]
    levels = lanes // piece
    items = lanes // chunk
    columns = owners * piece
    lat_rows = owners * rows_dev
    blocks = side.shape[0]
    half = blocks // 2
    buffers = leg_buf.shape[0]
    me = lax.axis_index("wave")

    load_x = pltpu.make_async_copy(x_hbm, x_ref, load_sem.at[0])
    load_x.start()

    def leg_copy(g):
        slot = lax.rem(g, buffers)
        return pltpu.make_async_copy(leg_hbm.at[g], leg_buf.at[slot], leg_sem.at[slot])

    def spec_copy(g):
        slot = lax.rem(g, 2)
        return pltpu.make_async_copy(spec_buf.at[slot], spec_hbm.at[g], spec_sem.at[slot])

    def out_copy(h, d):
        target = lax.rem(me + d, owners)
        return pltpu.make_async_remote_copy(
            src_ref=sent.at[h, target], dst_ref=recv.at[h, me],
            send_sem=fsend.at[h, d], recv_sem=frecv.at[h, d],
            device_id={"wave": target}, device_id_type=pl.DeviceIdType.MESH,
        )

    def in_copy(h, d):
        source = lax.rem(me + owners - d, owners)
        return pltpu.make_async_remote_copy(
            src_ref=sent.at[h, source], dst_ref=recv.at[h, source],
            send_sem=fsend.at[h, d], recv_sem=frecv.at[h, d],
            device_id={"wave": source}, device_id_type=pl.DeviceIdType.MESH,
        )

    def out_back(h, d):
        target = lax.rem(me + d, owners)
        return pltpu.make_async_remote_copy(
            src_ref=back.at[h, target], dst_ref=returned_hbm.at[h, me],
            send_sem=bsend.at[h, d], recv_sem=brecv.at[h, d],
            device_id={"wave": target}, device_id_type=pl.DeviceIdType.MESH,
        )

    def in_back(h, d):
        source = lax.rem(me + owners - d, owners)
        return pltpu.make_async_remote_copy(
            src_ref=back.at[h, source], dst_ref=returned_hbm.at[h, source],
            send_sem=bsend.at[h, d], recv_sem=brecv.at[h, d],
            device_id={"wave": source}, device_id_type=pl.DeviceIdType.MESH,
        )

    def own_back(h):
        return pltpu.make_async_copy(back.at[h, me], returned_hbm.at[h, me], own_sem.at[h])

    def loop(low, high, step):
        def body(i, carry):
            step(i)
            return carry

        lax.fori_loop(low, high, body, 0)

    barrier = pltpu.get_barrier_semaphore()

    def greet(d):
        pl.semaphore_signal(
            barrier, inc=1, device_id={"wave": lax.rem(me + d, owners)}, device_id_type=pl.DeviceIdType.MESH
        )

    loop(1, owners, greet)
    for g in range(buffers - 1):
        leg_copy(g).start()

    coarse = lon_cells // LANES

    def table_chunk(h):
        def rows_step(t):
            rows = pl.ds(pl.multiple_of(h * columns + t * 16, 16), 16)
            local = pl.ds(pl.multiple_of(t * 16, 16), 16)
            cos_lo = angles_ref[rows, 0:LANES]
            sin_lo = angles_ref[rows, LANES : 2 * LANES]
            high = angles_ref[rows, 2 * LANES : 2 * LANES + 2 * coarse]
            for b in range(coarse):
                value = high[:, b : b + 1] * cos_lo - high[:, coarse + b : coarse + b + 1] * sin_lo
                table_ref[h, local, b * LANES : (b + 1) * LANES] = value.astype(BF16)

        loop(0, columns // 16, rows_step)

    factor = 1.0 / math.sqrt(lon_cells)
    tile = 4 * rows_dev * 2

    def forward_chunk(h):
        table_chunk(h)

        @pl.when(h == 0)
        def _():
            load_x.wait()

        def dot_step(t):
            rows = pl.ds(pl.multiple_of(t * tile, tile), tile)
            y_ref[rows, :] = lax.dot_general(
                x_ref[rows, :], table_ref[h], (((1,), (1,)), ((), ())), preferred_element_type=F32
            ) * factor

        loop(0, levels * rows_dev // tile, dot_step)
        for w in range(owners):
            parts = [
                y_ref[k * rows_dev : (k + 1) * rows_dev, w * piece : (w + 1) * piece] for k in range(levels)
            ]
            sent[h, w] = jnp.concatenate(parts, axis=1).astype(BF16)

        @pl.when(h == 0)
        def _():
            pl.semaphore_wait(barrier, owners - 1)

        loop(1, owners, lambda d: out_copy(h, d).start())
        recv[h, me] = sent[h, me]

    loop(0, chunks, forward_chunk)
    save_table = pltpu.make_async_copy(table_ref, table_hbm, load_sem.at[1])
    save_table.start()

    wide = 128

    def middle_chunk(h):
        loop(1, owners, lambda d: in_copy(h, d).wait_recv())

        def unpack(t):
            cols = pl.ds(pl.multiple_of(t * wide, wide), wide)
            rows = recv[h, :, :, cols].astype(F32).reshape(lat_rows, wide).astype(BF16)
            value = lax.dot_general(
                rows, place_ref[...], (((0,), (0,)), ((), ())), preferred_element_type=F32
            )
            for b in range(blocks):
                side[b, cols, :] = value[:, b * LANES : (b + 1) * LANES]

        loop(0, lanes // wide, unpack)

        def slot_step(s):
            g = h * chunk + s

            @pl.when(g + buffers - 1 < slots)
            def _():
                leg_copy(g + buffers - 1).start()

            mine = pl.ds(s, items, stride=chunk)
            upper = jnp.concatenate([side[b, mine, :] for b in range(half)], axis=1)
            lower = jnp.concatenate([side[b, mine, :] for b in range(half, blocks)], axis=1)
            both = jnp.concatenate([upper, lower], axis=0)[:, :north].astype(BF16)
            leg_copy(g).wait()
            table = leg_buf[lax.rem(g, buffers)]
            result = jnp.dot(both, table, preferred_element_type=F32)
            offsets = lax.broadcasted_iota(jnp.int32, (1, total), 1) - wave_ref[g]
            sign = jnp.where(offsets % 2 == 0, 1.0, -1.0).astype(F32)
            spec = jnp.where(offsets >= 0, result[:items] + sign * result[items:], 0.0)

            @pl.when(g >= 2)
            def _():
                spec_copy(g - 2).wait()

            spec_buf[lax.rem(g, 2)] = spec.astype(BF16)
            spec_copy(g).start()
            filtered = (spec * spectrum_ref[...]).astype(BF16).astype(F32)
            second = jnp.concatenate([filtered, filtered * sign], axis=0).astype(BF16)
            folded = lax.dot_general(second, table, (((1,), (1,)), ((), ())), preferred_element_type=F32)
            folded = folded.astype(BF16).astype(F32)
            if half * LANES > north:
                pad = jnp.zeros((2 * items, half * LANES - north), F32)
                folded = jnp.concatenate([folded, pad], axis=1)
            for b in range(half):
                part = slice(b * LANES, (b + 1) * LANES)
                fold[b, mine, :] = folded[:items, part]
                fold[half + b, mine, :] = folded[items:, part]

        loop(0, chunk, slot_step)

        def pack(t):
            cols = pl.ds(pl.multiple_of(t * wide, wide), wide)
            value = jnp.concatenate([fold[b, cols, :] for b in range(blocks)], axis=1).astype(BF16)
            rows = lax.dot_general(
                place_ref[...], value, (((1,), (1,)), ((), ())), preferred_element_type=F32
            )
            back[h, :, :, cols] = rows.reshape(owners, rows_dev, wide).astype(BF16)

        loop(0, lanes // wide, pack)
        loop(1, owners, lambda d: out_back(h, d).start())
        own_back(h).start()

    loop(0, chunks, middle_chunk)
    spec_copy(slots - 2).wait()
    spec_copy(slots - 1).wait()
    save_table.wait()

    def finish(h):
        loop(1, owners, lambda d: out_copy(h, d).wait_send())
        loop(1, owners, lambda d: out_back(h, d).wait_send())
        loop(1, owners, lambda d: in_back(h, d).wait_recv())
        own_back(h).wait()

    loop(0, chunks, finish)


def exchange(chunks, owners, rows_dev, mine, x, angles, place, table, spectrum):
    slots, north, total = table.shape
    lon_cells = x.shape[1]
    levels = x.shape[0] // rows_dev
    chunk = slots // chunks
    lanes = 2 * levels * chunk
    columns = owners * 2 * chunk
    blocks = place.shape[1] // LANES
    hbm = pl.BlockSpec(memory_space=pl.ANY)
    vmem = pl.BlockSpec(memory_space=pltpu.VMEM)
    block = (chunks, owners, rows_dev, lanes)
    sems = pltpu.SemaphoreType.DMA
    return pl.pallas_call(
        functools.partial(exchange_body, owners, chunks),
        in_specs=[pl.BlockSpec(memory_space=pltpu.SMEM), hbm, vmem, vmem, hbm, vmem],
        out_specs=[hbm, hbm, hbm],
        out_shape=[
            jax.ShapeDtypeStruct((slots, 2 * levels, total), BF16),
            jax.ShapeDtypeStruct(block, BF16),
            jax.ShapeDtypeStruct((chunks, columns, lon_cells), BF16),
        ],
        scratch_shapes=[
            pltpu.VMEM(x.shape, BF16),
            pltpu.VMEM((chunks, columns, lon_cells), BF16),
            pltpu.VMEM((x.shape[0], columns), F32),
            pltpu.VMEM(block, BF16),
            pltpu.VMEM(block, BF16),
            pltpu.VMEM(block, BF16),
            pltpu.VMEM((blocks, lanes, LANES), F32),
            pltpu.VMEM((blocks, lanes, LANES), F32),
            pltpu.VMEM((4, north, total), BF16),
            pltpu.VMEM((2, 2 * levels, total), BF16),
            sems((chunks, owners)),
            sems((chunks, owners)),
            sems((chunks, owners)),
            sems((chunks, owners)),
            sems((2,)),
            sems((4,)),
            sems((2,)),
            sems((chunks,)),
        ],
        compiler_params=params(collective_id=0, has_side_effects=True),
        cost_estimate=pl.CostEstimate(
            flops=2 * x.size * columns * chunks + 8 * slots * north * total * 2 * levels,
            bytes_accessed=2 * (x.size + table.size) + 8 * x.size,
            transcendentals=0,
        ),
        name="fourier_legendre_exchange",
    )(mine, x, angles, place, table, spectrum)


def inverse_body(rows_dev, group, piece, factor, returned_ref, table_ref, out_ref):
    chunks, owners = returned_ref.shape[:2]
    total = None
    for h in range(chunks):
        blocks = [returned_ref[h, w].astype(F32) for w in range(owners)]
        rows = [
            jnp.concatenate([b[:, k * piece : (k + 1) * piece] for b in blocks], axis=1)
            for k in range(group)
        ]
        z = jnp.concatenate(rows, axis=0).astype(BF16)
        term = jnp.dot(z, table_ref[h], preferred_element_type=F32)
        total = term if total is None else total + term
    out_ref[...] = (total * factor).astype(BF16)


def inverse(returned, tables, waves_count):
    chunks, owners, rows_dev, lanes = returned.shape
    columns, lon_cells = tables.shape[1:]
    piece = columns // owners
    items = lanes // piece
    group = LANES // math.gcd(piece, LANES)
    body = functools.partial(inverse_body, rows_dev, group, piece, 1.0 / math.sqrt(waves_count))
    return pl.pallas_call(
        body,
        grid=(items // group,),
        in_specs=[
            pl.BlockSpec((chunks, owners, rows_dev, group * piece), lambda g: (0, 0, 0, g)),
            pl.BlockSpec(tables.shape, lambda g: (0, 0, 0)),
        ],
        out_specs=pl.BlockSpec((group * rows_dev, lon_cells), lambda g: (g, 0)),
        out_shape=jax.ShapeDtypeStruct((items * rows_dev, lon_cells), BF16),
        compiler_params=params(),
        name="inverse_fourier",
    )(returned, tables)


def kernels_fit(owners, items, rows_dev, slots, north, total, lon_cells):
    chunk = slots // PARTS
    piece = 2 * chunk
    group = LANES // math.gcd(piece, LANES)
    return (
        slots % PARTS == 0
        and rows_dev % 8 == 0
        and items % 8 == 0
        and items % group == 0
        and total % LANES == 0
        and lon_cells % (4 * LANES) == 0
        and owners * piece % 16 == 0
        and slots > 4
    )


def local_kernels(grid_grad, legendre, spectrum, owner_waves, lat_order):
    owners = lax.axis_size("wave")
    items, rows_dev, lon_cells = grid_grad.shape
    slots, total, north = legendre.shape
    waves = owner_waves.reshape(owners, slots)
    mine = lax.dynamic_index_in_dim(waves, lax.axis_index("wave"), 0, keepdims=False)
    x = grid_grad.reshape(items * rows_dev, lon_cells)
    table = jnp.swapaxes(legendre, 1, 2)
    half = up(north, LANES)
    column = jnp.where(lat_order < north, lat_order, lat_order - north + half)
    place = (column[:, None] == lax.iota(jnp.int32, 2 * half)[None, :]).astype(BF16)
    in_chunks = jnp.swapaxes(waves.reshape(owners, PARTS, slots // PARTS), 0, 1)
    angles = angle_tables(in_chunks, lon_cells)
    spec, returned, phases = exchange(
        PARTS, owners, rows_dev, mine, x, angles, place, table, spectrum[None, :]
    )
    smoothed = inverse(returned, phases, owners * slots)
    return (spec, smoothed.reshape(grid_grad.shape))


def phase_table(waves, lon_cells, factor):
    ticks = lax.iota(jnp.int32, lon_cells)
    turns = waves[..., None] * ticks % lon_cells
    angle = turns.astype(jnp.float32) * (2.0 * math.pi / lon_cells)
    return jnp.stack([jnp.cos(angle), -jnp.sin(angle)], axis=1) * factor


def split_table(table):
    high_part = table.astype(jnp.bfloat16)
    low_part = (table - high_part.astype(jnp.float32)).astype(jnp.bfloat16)
    return (high_part, low_part)


def row_signs(count, wave):
    offsets = lax.iota(jnp.int32, count) - wave[..., None]
    return ((1 - 2 * (offsets % 2)).astype(jnp.float32), offsets >= 0)


def legendre_padded(legendre, side, spectrum, mine):
    half = side.shape[2] // 2
    result = jnp.einsum("snj,sjc->scn", legendre, side, preferred_element_type=jnp.float32)
    sign, valid = row_signs(legendre.shape[1], mine)
    spec = jnp.where(valid[:, None, :], result[:, :half] + sign[:, None, :] * result[:, half:], 0.0)
    filtered = (spec * spectrum).astype(jnp.bfloat16)
    second = jnp.concatenate([filtered, filtered * sign[:, None, :].astype(jnp.bfloat16)], axis=1)
    folded = jnp.einsum("snj,scn->scj", legendre, second, preferred_element_type=jnp.float32)
    return (spec, folded)


def local_plain(grid_grad, legendre, spectrum, owner_waves, lat_order):
    owners = lax.axis_size("wave")
    fields_levels, rows_dev, lon_cells = grid_grad.shape
    slots, total_rows, north_rows = legendre.shape
    lat_rows = rows_dev * owners
    waves = owner_waves.reshape(owners, slots)
    mine = lax.dynamic_index_in_dim(waves, lax.axis_index("wave"), 0, keepdims=False)
    forward_high, forward_low = split_table(
        phase_table(waves, lon_cells, 1.0 / math.sqrt(lon_cells))
    )
    inverse_high, inverse_low = split_table(
        phase_table(waves, lon_cells, 1.0 / math.sqrt(owners * slots))
    )
    onehot = (lat_order[None, :] == lax.iota(jnp.int32, lat_rows)[:, None]).astype(jnp.bfloat16)
    onehot = onehot.reshape(2, north_rows, owners, rows_dev)
    fourier = jnp.einsum(
        "kri,wpsi->wkrps", grid_grad, forward_high, preferred_element_type=jnp.float32
    )
    fourier = fourier + jnp.einsum(
        "kri,wpsi->wkrps", grid_grad, forward_low, preferred_element_type=jnp.float32
    )
    fourier = fourier.astype(jnp.bfloat16).reshape(owners, fields_levels, rows_dev, 2 * slots)
    received = lax.all_to_all(fourier, "wave", split_axis=0, concat_axis=0, tiled=True)
    items = received.shape[1]
    split = received.reshape(owners, items, rows_dev, 2, slots)
    side = jnp.einsum("hjwr,wkrps->sjhkp", onehot, split, preferred_element_type=jnp.float32)
    side = side.astype(jnp.bfloat16).reshape(slots, north_rows, 4 * items)
    spec, folded = legendre_padded(legendre, side, spectrum, mine)
    folded = folded.astype(jnp.bfloat16).reshape(slots, 2, items, 2, north_rows)
    back = jnp.einsum("hjwr,shkpj->wkrps", onehot, folded, preferred_element_type=jnp.float32)
    back = back.astype(jnp.bfloat16).reshape(owners, items, rows_dev, 2 * slots)
    returned = lax.all_to_all(back, "wave", split_axis=0, concat_axis=0, tiled=True)
    spec_out = spec.reshape(slots, items, 2, total_rows).astype(jnp.bfloat16)
    spec_out, returned = (spec_out, returned)
    gradient_spectra = spec_out.reshape(slots, 2 * fields_levels, total_rows)
    returned = returned.reshape(owners, fields_levels, rows_dev, 2, slots)
    smoothed = jnp.einsum(
        "wkrps,wpsi->kri", returned, inverse_high, preferred_element_type=jnp.float32
    )
    smoothed = smoothed + jnp.einsum(
        "wkrps,wpsi->kri", returned, inverse_low, preferred_element_type=jnp.float32
    )
    return (gradient_spectra, smoothed.astype(jnp.bfloat16))


def local(grid_grad, legendre, spectrum, owner_waves, lat_order):
    slots, total, north = legendre.shape
    if kernels_fit(lax.axis_size("wave"), *grid_grad.shape[:2], slots, north, total, grid_grad.shape[2]):
        return local_kernels(grid_grad, legendre, spectrum, owner_waves, lat_order)
    return local_plain(grid_grad, legendre, spectrum, owner_waves, lat_order)


def solution(mesh):
    in_specs = (P("members", "wave", None), P("wave", None, None), P(), P(), P())
    out_specs = (P(("members", "wave"), None, None), P("members", "wave", None))
    return jax.shard_map(local, mesh=mesh, in_specs=in_specs, out_specs=out_specs, check_vma=False)
```

```python
import functools
import math

import jax
import ml_dtypes
import numpy as np
import jax.numpy as jnp
from jax import lax
from jax.experimental import pallas as pl
from jax.experimental.pallas import tpu as pltpu
from jax.sharding import PartitionSpec as P

LANES = 128
PARTS = 4
VMEM = 62 * 2**20
F32 = jnp.float32
BF16 = jnp.bfloat16


def up(value, step):
    return -(-value // step) * step


def params(**extra):
    return pltpu.CompilerParams(vmem_limit_bytes=VMEM, **extra)


def phase_constants(count, lon_cells):
    turns = np.arange(count)[:, None] * np.arange(lon_cells)[None, :] % lon_cells
    angle = turns * (2.0 * np.pi / lon_cells)
    return np.concatenate([np.cos(angle), -np.sin(angle)], axis=0).astype(ml_dtypes.bfloat16)


def exchange_body(
    owners, chunks, wave_ref, x_hbm, phase_hbm, pick_ref, column_ref, leg_hbm, spectrum_ref,
    spec_hbm, smooth_hbm,
    x_ref, phase_ref, table_ref, y_ref, total_ref, place_ref,
    sent, recv, back, returned, side, fold, leg_buf, spec_buf,
    fsend, frecv, bsend, brecv, load_sem, leg_sem, spec_sem, smooth_sem,
):
    slots, north, total = leg_hbm.shape
    lon_cells = x_hbm.shape[1]
    chunk = slots // chunks
    piece = 2 * chunk
    rows_dev = sent.shape[2]
    lanes = sent.shape[3]
    levels = lanes // piece
    items = lanes // chunk
    columns = owners * piece
    lat_rows = owners * rows_dev
    blocks = side.shape[0]
    half = blocks // 2
    buffers = leg_buf.shape[0]
    me = lax.axis_index("wave")

    load_x = pltpu.make_async_copy(x_hbm, x_ref, load_sem.at[0])
    load_phase = pltpu.make_async_copy(phase_hbm, phase_ref, load_sem.at[1])
    load_phase.start()
    load_x.start()

    def leg_copy(g):
        slot = lax.rem(g, buffers)
        return pltpu.make_async_copy(leg_hbm.at[g], leg_buf.at[slot], leg_sem.at[slot])

    def spec_copy(g):
        slot = lax.rem(g, 2)
        return pltpu.make_async_copy(spec_buf.at[slot], spec_hbm.at[g], spec_sem.at[slot])

    def out_copy(h, d):
        target = lax.rem(me + d, owners)
        return pltpu.make_async_remote_copy(
            src_ref=sent.at[h, target], dst_ref=recv.at[h, me],
            send_sem=fsend.at[h, d], recv_sem=frecv.at[h, d],
            device_id={"wave": target}, device_id_type=pl.DeviceIdType.MESH,
        )

    def in_copy(h, d):
        source = lax.rem(me + owners - d, owners)
        return pltpu.make_async_remote_copy(
            src_ref=sent.at[h, source], dst_ref=recv.at[h, source],
            send_sem=fsend.at[h, d], recv_sem=frecv.at[h, d],
            device_id={"wave": source}, device_id_type=pl.DeviceIdType.MESH,
        )

    def out_back(h, d):
        target = lax.rem(me + d, owners)
        return pltpu.make_async_remote_copy(
            src_ref=back.at[h, target], dst_ref=returned.at[h, me],
            send_sem=bsend.at[h, d], recv_sem=brecv.at[h, d],
            device_id={"wave": target}, device_id_type=pl.DeviceIdType.MESH,
        )

    def in_back(h, d):
        source = lax.rem(me + owners - d, owners)
        return pltpu.make_async_remote_copy(
            src_ref=back.at[h, source], dst_ref=returned.at[h, source],
            send_sem=bsend.at[h, d], recv_sem=brecv.at[h, d],
            device_id={"wave": source}, device_id_type=pl.DeviceIdType.MESH,
        )

    def loop(low, high, step):
        def body(i, carry):
            step(i)
            return carry

        lax.fori_loop(low, high, body, 0)

    barrier = pltpu.get_barrier_semaphore()

    def greet(d):
        pl.semaphore_signal(
            barrier, inc=1, device_id={"wave": lax.rem(me + d, owners)}, device_id_type=pl.DeviceIdType.MESH
        )

    loop(1, owners, greet)
    for g in range(buffers - 1):
        leg_copy(g).start()

    place_ref[...] = jnp.where(
        lax.broadcasted_iota(jnp.int32, place_ref.shape, 0) == column_ref[...], 1.0, 0.0
    ).astype(BF16)
    load_phase.wait()

    def table_chunk(h):
        rows = lax.broadcasted_iota(jnp.int32, (phase_ref.shape[0], columns), 0)
        pick = jnp.where(rows == pick_ref[h], 1.0, 0.0).astype(BF16)

        def lon_step(t):
            cells = pl.ds(pl.multiple_of(t * 512, 512), 512)
            table_ref[h, :, cells] = lax.dot_general(
                pick, phase_ref[:, cells], (((0,), (0,)), ((), ())), preferred_element_type=F32
            ).astype(BF16)

        loop(0, lon_cells // 512, lon_step)

    factor = 1.0 / math.sqrt(lon_cells)
    tile = 4 * rows_dev * 2

    def forward_chunk(h):
        table_chunk(h)

        @pl.when(h == 0)
        def _():
            load_x.wait()

        def dot_step(t):
            rows = pl.ds(pl.multiple_of(t * tile, tile), tile)
            y_ref[rows, :] = lax.dot_general(
                x_ref[rows, :], table_ref[h], (((1,), (1,)), ((), ())), preferred_element_type=F32
            ) * factor

        loop(0, levels * rows_dev // tile, dot_step)
        for w in range(owners):
            parts = [
                y_ref[k * rows_dev : (k + 1) * rows_dev, w * piece : (w + 1) * piece] for k in range(levels)
            ]
            sent[h, w] = jnp.concatenate(parts, axis=1).astype(BF16)

        @pl.when(h == 0)
        def _():
            pl.semaphore_wait(barrier, owners - 1)

        loop(1, owners, lambda d: out_copy(h, d).start())
        recv[h, me] = sent[h, me]

    loop(0, chunks, forward_chunk)
    wide = 128

    def middle_chunk(h):
        loop(1, owners, lambda d: in_copy(h, d).wait_recv())

        def unpack(t):
            cols = pl.ds(pl.multiple_of(t * wide, wide), wide)
            rows = recv[h, :, :, cols].astype(F32).reshape(lat_rows, wide).astype(BF16)
            value = lax.dot_general(
                rows, place_ref[...], (((0,), (1,)), ((), ())), preferred_element_type=F32
            )
            for b in range(blocks):
                side[b, cols, :] = value[:, b * LANES : (b + 1) * LANES]

        loop(0, lanes // wide, unpack)

        def slot_step(s):
            g = h * chunk + s

            @pl.when(g + buffers - 1 < slots)
            def _():
                leg_copy(g + buffers - 1).start()

            mine = pl.ds(s, items, stride=chunk)
            upper = jnp.concatenate([side[b, mine, :] for b in range(half)], axis=1)
            lower = jnp.concatenate([side[b, mine, :] for b in range(half, blocks)], axis=1)
            both = jnp.concatenate([upper, lower], axis=0)[:, :north].astype(BF16)
            leg_copy(g).wait()
            table = leg_buf[lax.rem(g, buffers)]
            result = jnp.dot(both, table, preferred_element_type=F32)
            offsets = lax.broadcasted_iota(jnp.int32, (1, total), 1) - wave_ref[me * slots + g]
            sign = jnp.where(offsets % 2 == 0, 1.0, -1.0).astype(F32)
            spec = jnp.where(offsets >= 0, result[:items] + sign * result[items:], 0.0)

            @pl.when(g >= 2)
            def _():
                spec_copy(g - 2).wait()

            spec_buf[lax.rem(g, 2)] = spec.astype(BF16)
            spec_copy(g).start()
            filtered = (spec * spectrum_ref[...]).astype(BF16).astype(F32)
            second = jnp.concatenate([filtered, filtered * sign], axis=0).astype(BF16)
            folded = lax.dot_general(second, table, (((1,), (1,)), ((), ())), preferred_element_type=F32)
            folded = folded.astype(BF16).astype(F32)
            if half * LANES > north:
                pad = jnp.zeros((2 * items, half * LANES - north), F32)
                folded = jnp.concatenate([folded, pad], axis=1)
            for b in range(half):
                part = slice(b * LANES, (b + 1) * LANES)
                fold[b, mine, :] = folded[:items, part]
                fold[half + b, mine, :] = folded[items:, part]

        loop(0, chunk, slot_step)

        def pack(t):
            cols = pl.ds(pl.multiple_of(t * wide, wide), wide)
            value = jnp.concatenate([fold[b, cols, :] for b in range(blocks)], axis=1).astype(BF16)
            rows = lax.dot_general(
                place_ref[...], value, (((0,), (1,)), ((), ())), preferred_element_type=F32
            )
            back[h, :, :, cols] = rows.reshape(owners, rows_dev, wide).astype(BF16)

        loop(0, lanes // wide, pack)
        loop(1, owners, lambda d: out_back(h, d).start())
        returned[h, me] = back[h, me]

    loop(0, chunks, middle_chunk)
    spec_copy(slots - 2).wait()
    spec_copy(slots - 1).wait()

    scale = 1.0 / math.sqrt(owners * slots)
    tiles = levels * rows_dev // tile

    def smooth_copy(t):
        rows = pl.ds(pl.multiple_of(t * tile, tile), tile)
        return pltpu.make_async_copy(x_ref.at[rows], smooth_hbm.at[rows], smooth_sem.at[t])

    def inverse_chunk(h):
        loop(1, owners, lambda d: in_back(h, d).wait_recv())
        for k in range(levels):
            parts = [
                returned[h, w, :, k * piece : (k + 1) * piece].astype(F32) for w in range(owners)
            ]
            y_ref[k * rows_dev : (k + 1) * rows_dev, :] = jnp.concatenate(parts, axis=1)

        def dot_step(t):
            rows = pl.ds(pl.multiple_of(t * tile, tile), tile)
            term = jnp.dot(y_ref[rows, :].astype(BF16), table_ref[h], preferred_element_type=F32)

            @pl.when(h == 0)
            def _():
                total_ref[rows, :] = term

            @pl.when(jnp.logical_and(h > 0, h < chunks - 1))
            def _():
                total_ref[rows, :] += term

            @pl.when(h == chunks - 1)
            def _():
                x_ref[rows, :] = ((total_ref[rows, :] + term) * scale).astype(BF16)
                smooth_copy(t).start()

        loop(0, tiles, dot_step)

    loop(0, chunks, inverse_chunk)

    def finish(h):
        loop(1, owners, lambda d: out_copy(h, d).wait_send())
        loop(1, owners, lambda d: out_back(h, d).wait_send())

    loop(0, chunks, finish)
    loop(0, tiles, lambda t: smooth_copy(t).wait())


def exchange(chunks, owners, rows_dev, waves, x, phases, picks, column, table, spectrum):
    slots, north, total = table.shape
    lon_cells = x.shape[1]
    levels = x.shape[0] // rows_dev
    chunk = slots // chunks
    lanes = 2 * levels * chunk
    columns = owners * 2 * chunk
    lat_rows = owners * rows_dev
    blocks = 2 * up(north, LANES) // LANES
    tiles = levels // 8
    hbm = pl.BlockSpec(memory_space=pl.ANY)
    vmem = pl.BlockSpec(memory_space=pltpu.VMEM)
    block = (chunks, owners, rows_dev, lanes)
    sems = pltpu.SemaphoreType.DMA
    return pl.pallas_call(
        functools.partial(exchange_body, owners, chunks),
        in_specs=[pl.BlockSpec(memory_space=pltpu.SMEM), hbm, hbm, vmem, vmem, hbm, vmem],
        out_specs=[hbm, hbm],
        out_shape=[
            jax.ShapeDtypeStruct((slots, 2 * levels, total), BF16),
            jax.ShapeDtypeStruct(x.shape, BF16),
        ],
        scratch_shapes=[
            pltpu.VMEM(x.shape, BF16),
            pltpu.VMEM(phases.shape, BF16),
            pltpu.VMEM((chunks, columns, lon_cells), BF16),
            pltpu.VMEM((x.shape[0], columns), F32),
            pltpu.VMEM(x.shape, F32),
            pltpu.VMEM((blocks * LANES, lat_rows), BF16),
            pltpu.VMEM(block, BF16),
            pltpu.VMEM(block, BF16),
            pltpu.VMEM(block, BF16),
            pltpu.VMEM(block, BF16),
            pltpu.VMEM((blocks, lanes, LANES), F32),
            pltpu.VMEM((blocks, lanes, LANES), F32),
            pltpu.VMEM((4, north, total), BF16),
            pltpu.VMEM((2, 2 * levels, total), BF16),
            sems((chunks, owners)),
            sems((chunks, owners)),
            sems((chunks, owners)),
            sems((chunks, owners)),
            sems((2,)),
            sems((4,)),
            sems((2,)),
            sems((tiles,)),
        ],
        compiler_params=params(collective_id=0, has_side_effects=True),
        cost_estimate=pl.CostEstimate(
            flops=2 * x.size * columns * chunks + 8 * slots * north * total * 2 * levels,
            bytes_accessed=2 * (x.size + table.size) + 8 * x.size,
            transcendentals=0,
        ),
        name="fourier_legendre_exchange",
    )(waves, x, phases, picks, column, table, spectrum)


def kernels_fit(owners, items, rows_dev, slots, north, total, lon_cells):
    chunk = slots // PARTS
    piece = 2 * chunk
    group = LANES // math.gcd(piece, LANES)
    return (
        slots % PARTS == 0
        and rows_dev % 8 == 0
        and items % 8 == 0
        and items % group == 0
        and total % LANES == 0
        and lon_cells % 512 == 0
        and owners * piece % 16 == 0
        and slots > 4
    )


def local_kernels(grid_grad, legendre, spectrum, owner_waves, lat_order):
    owners = lax.axis_size("wave")
    items, rows_dev, lon_cells = grid_grad.shape
    slots, total, north = legendre.shape
    waves = owner_waves.reshape(owners, slots)
    x = grid_grad.reshape(items * rows_dev, lon_cells)
    table = jnp.swapaxes(legendre, 1, 2)
    half = up(north, LANES)
    column = jnp.where(lat_order < north, lat_order, lat_order - north + half)[None, :]
    chunk = slots // PARTS
    in_chunks = jnp.swapaxes(waves.reshape(owners, PARTS, chunk), 0, 1)
    picks = jnp.stack([in_chunks, in_chunks + owners * slots], axis=2).reshape(PARTS, 1, -1)
    phases = jnp.asarray(phase_constants(owners * slots, lon_cells))
    spec, smoothed = exchange(
        PARTS, owners, rows_dev, owner_waves, x, phases, picks, column, table, spectrum[None, :]
    )
    return (spec, smoothed.reshape(grid_grad.shape))


def phase_table(waves, lon_cells, factor):
    ticks = lax.iota(jnp.int32, lon_cells)
    turns = waves[..., None] * ticks % lon_cells
    angle = turns.astype(jnp.float32) * (2.0 * math.pi / lon_cells)
    return jnp.stack([jnp.cos(angle), -jnp.sin(angle)], axis=1) * factor


def split_table(table):
    high_part = table.astype(jnp.bfloat16)
    low_part = (table - high_part.astype(jnp.float32)).astype(jnp.bfloat16)
    return (high_part, low_part)


def row_signs(count, wave):
    offsets = lax.iota(jnp.int32, count) - wave[..., None]
    return ((1 - 2 * (offsets % 2)).astype(jnp.float32), offsets >= 0)


def legendre_padded(legendre, side, spectrum, mine):
    half = side.shape[2] // 2
    result = jnp.einsum("snj,sjc->scn", legendre, side, preferred_element_type=jnp.float32)
    sign, valid = row_signs(legendre.shape[1], mine)
    spec = jnp.where(valid[:, None, :], result[:, :half] + sign[:, None, :] * result[:, half:], 0.0)
    filtered = (spec * spectrum).astype(jnp.bfloat16)
    second = jnp.concatenate([filtered, filtered * sign[:, None, :].astype(jnp.bfloat16)], axis=1)
    folded = jnp.einsum("snj,scn->scj", legendre, second, preferred_element_type=jnp.float32)
    return (spec, folded)


def local_plain(grid_grad, legendre, spectrum, owner_waves, lat_order):
    owners = lax.axis_size("wave")
    fields_levels, rows_dev, lon_cells = grid_grad.shape
    slots, total_rows, north_rows = legendre.shape
    lat_rows = rows_dev * owners
    waves = owner_waves.reshape(owners, slots)
    mine = lax.dynamic_index_in_dim(waves, lax.axis_index("wave"), 0, keepdims=False)
    forward_high, forward_low = split_table(
        phase_table(waves, lon_cells, 1.0 / math.sqrt(lon_cells))
    )
    inverse_high, inverse_low = split_table(
        phase_table(waves, lon_cells, 1.0 / math.sqrt(owners * slots))
    )
    onehot = (lat_order[None, :] == lax.iota(jnp.int32, lat_rows)[:, None]).astype(jnp.bfloat16)
    onehot = onehot.reshape(2, north_rows, owners, rows_dev)
    fourier = jnp.einsum(
        "kri,wpsi->wkrps", grid_grad, forward_high, preferred_element_type=jnp.float32
    )
    fourier = fourier + jnp.einsum(
        "kri,wpsi->wkrps", grid_grad, forward_low, preferred_element_type=jnp.float32
    )
    fourier = fourier.astype(jnp.bfloat16).reshape(owners, fields_levels, rows_dev, 2 * slots)
    received = lax.all_to_all(fourier, "wave", split_axis=0, concat_axis=0, tiled=True)
    items = received.shape[1]
    split = received.reshape(owners, items, rows_dev, 2, slots)
    side = jnp.einsum("hjwr,wkrps->sjhkp", onehot, split, preferred_element_type=jnp.float32)
    side = side.astype(jnp.bfloat16).reshape(slots, north_rows, 4 * items)
    spec, folded = legendre_padded(legendre, side, spectrum, mine)
    folded = folded.astype(jnp.bfloat16).reshape(slots, 2, items, 2, north_rows)
    back = jnp.einsum("hjwr,shkpj->wkrps", onehot, folded, preferred_element_type=jnp.float32)
    back = back.astype(jnp.bfloat16).reshape(owners, items, rows_dev, 2 * slots)
    returned = lax.all_to_all(back, "wave", split_axis=0, concat_axis=0, tiled=True)
    spec_out = spec.reshape(slots, items, 2, total_rows).astype(jnp.bfloat16)
    spec_out, returned = (spec_out, returned)
    gradient_spectra = spec_out.reshape(slots, 2 * fields_levels, total_rows)
    returned = returned.reshape(owners, fields_levels, rows_dev, 2, slots)
    smoothed = jnp.einsum(
        "wkrps,wpsi->kri", returned, inverse_high, preferred_element_type=jnp.float32
    )
    smoothed = smoothed + jnp.einsum(
        "wkrps,wpsi->kri", returned, inverse_low, preferred_element_type=jnp.float32
    )
    return (gradient_spectra, smoothed.astype(jnp.bfloat16))


def local(grid_grad, legendre, spectrum, owner_waves, lat_order):
    slots, total, north = legendre.shape
    if kernels_fit(lax.axis_size("wave"), *grid_grad.shape[:2], slots, north, total, grid_grad.shape[2]):
        return local_kernels(grid_grad, legendre, spectrum, owner_waves, lat_order)
    return local_plain(grid_grad, legendre, spectrum, owner_waves, lat_order)


def solution(mesh):
    in_specs = (P("members", "wave", None), P("wave", None, None), P(), P(), P())
    out_specs = (P(("members", "wave"), None, None), P("members", "wave", None))
    return jax.shard_map(local, mesh=mesh, in_specs=in_specs, out_specs=out_specs, check_vma=False)
```

```python
import functools
import math

import jax
import ml_dtypes
import numpy as np
import jax.numpy as jnp
from jax import lax
from jax.experimental import pallas as pl
from jax.experimental.pallas import tpu as pltpu
from jax.sharding import PartitionSpec as P

LANES = 128
PARTS = 4
VMEM = 62 * 2**20
F32 = jnp.float32
BF16 = jnp.bfloat16


def up(value, step):
    return -(-value // step) * step


def params(**extra):
    return pltpu.CompilerParams(vmem_limit_bytes=VMEM, **extra)


def phase_constants(count, lon_cells):
    turns = np.arange(count)[:, None] * np.arange(lon_cells)[None, :] % lon_cells
    angle = turns * (2.0 * np.pi / lon_cells)
    return np.concatenate([np.cos(angle), -np.sin(angle)], axis=0).astype(ml_dtypes.bfloat16)


def exchange_body(
    owners, chunks, wave_ref, x_hbm, phase_hbm, pick_ref, lat_ref, leg_hbm, spectrum_ref,
    spec_hbm, smooth_hbm,
    x_ref, phase_ref, table_ref, y_ref, total_ref, place_ref,
    sent, recv, back, returned, side, fold, leg_buf, spec_buf,
    fsend, frecv, bsend, brecv, load_sem, leg_sem, spec_sem, smooth_sem,
):
    slots, north, total = leg_hbm.shape
    lon_cells = x_hbm.shape[1]
    chunk = slots // chunks
    piece = 2 * chunk
    rows_dev = sent.shape[2]
    lanes = sent.shape[3]
    levels = lanes // piece
    items = lanes // chunk
    columns = owners * piece
    lat_rows = owners * rows_dev
    blocks = side.shape[0]
    half = blocks // 2
    buffers = leg_buf.shape[0]
    me = lax.axis_index("wave")

    load_x = pltpu.make_async_copy(x_hbm, x_ref, load_sem.at[0])
    load_phase = pltpu.make_async_copy(phase_hbm, phase_ref, load_sem.at[1])
    load_phase.start()
    load_x.start()

    def leg_copy(g):
        slot = lax.rem(g, buffers)
        return pltpu.make_async_copy(leg_hbm.at[g], leg_buf.at[slot], leg_sem.at[slot])

    def spec_copy(g):
        slot = lax.rem(g, 2)
        return pltpu.make_async_copy(spec_buf.at[slot], spec_hbm.at[g], spec_sem.at[slot])

    def out_copy(h, d):
        target = lax.rem(me + d, owners)
        return pltpu.make_async_remote_copy(
            src_ref=sent.at[h, target], dst_ref=recv.at[h, me],
            send_sem=fsend.at[h, d], recv_sem=frecv.at[h, d],
            device_id={"wave": target}, device_id_type=pl.DeviceIdType.MESH,
        )

    def in_copy(h, d):
        source = lax.rem(me + owners - d, owners)
        return pltpu.make_async_remote_copy(
            src_ref=sent.at[h, source], dst_ref=recv.at[h, source],
            send_sem=fsend.at[h, d], recv_sem=frecv.at[h, d],
            device_id={"wave": source}, device_id_type=pl.DeviceIdType.MESH,
        )

    def out_back(h, d):
        target = lax.rem(me + d, owners)
        return pltpu.make_async_remote_copy(
            src_ref=back.at[h, target], dst_ref=returned.at[h, me],
            send_sem=bsend.at[h, d], recv_sem=brecv.at[h, d],
            device_id={"wave": target}, device_id_type=pl.DeviceIdType.MESH,
        )

    def in_back(h, d):
        source = lax.rem(me + owners - d, owners)
        return pltpu.make_async_remote_copy(
            src_ref=back.at[h, source], dst_ref=returned.at[h, source],
            send_sem=bsend.at[h, d], recv_sem=brecv.at[h, d],
            device_id={"wave": source}, device_id_type=pl.DeviceIdType.MESH,
        )

    def loop(low, high, step):
        def body(i, carry):
            step(i)
            return carry

        lax.fori_loop(low, high, body, 0)

    middle = owners // 2

    def far_first(i):
        return middle + (i // 2) * (1 - 2 * (i % 2))

    barrier = pltpu.get_barrier_semaphore()

    def greet(d):
        pl.semaphore_signal(
            barrier, inc=1, device_id={"wave": lax.rem(me + d, owners)}, device_id_type=pl.DeviceIdType.MESH
        )

    loop(1, owners, greet)
    lat = lat_ref[...].reshape(1, lat_rows)
    column = jnp.where(lat < north, lat, lat - north + half * LANES)
    place_ref[...] = jnp.where(
        lax.broadcasted_iota(jnp.int32, place_ref.shape, 0) == column, 1.0, 0.0
    ).astype(BF16)
    load_phase.wait()

    def table_chunk(h):
        rows = lax.broadcasted_iota(jnp.int32, (phase_ref.shape[0], columns), 0)
        pick = jnp.where(rows == pick_ref[h], 1.0, 0.0).astype(BF16)

        def lon_step(t):
            cells = pl.ds(pl.multiple_of(t * 512, 512), 512)
            table_ref[h, :, cells] = lax.dot_general(
                pick, phase_ref[:, cells], (((0,), (0,)), ((), ())), preferred_element_type=F32
            ).astype(BF16)

        loop(0, lon_cells // 512, lon_step)

    factor = 1.0 / math.sqrt(lon_cells)
    tile = 4 * rows_dev * 2

    def forward_chunk(h):
        table_chunk(h)

        @pl.when(h == 0)
        def _():
            load_x.wait()

        def dot_step(t):
            rows = pl.ds(pl.multiple_of(t * tile, tile), tile)
            y_ref[rows, :] = lax.dot_general(
                x_ref[rows, :], table_ref[h], (((1,), (1,)), ((), ())), preferred_element_type=F32
            ) * factor

        loop(0, levels * rows_dev // tile, dot_step)
        for w in range(owners):
            parts = [
                y_ref[k * rows_dev : (k + 1) * rows_dev, w * piece : (w + 1) * piece] for k in range(levels)
            ]
            sent[h, w] = jnp.concatenate(parts, axis=1).astype(BF16)

        @pl.when(h == 0)
        def _():
            pl.semaphore_wait(barrier, owners - 1)

        loop(1, owners, lambda i: out_copy(h, far_first(i)).start())
        recv[h, me] = sent[h, me]

    loop(0, chunks, forward_chunk)
    for g in range(buffers - 1):
        leg_copy(g).start()

    wide = 128

    def middle_chunk(h):
        loop(1, owners, lambda d: in_copy(h, d).wait_recv())

        def unpack(t):
            cols = pl.ds(pl.multiple_of(t * wide, wide), wide)
            rows = recv[h, :, :, cols].astype(F32).reshape(lat_rows, wide).astype(BF16)
            value = lax.dot_general(
                rows, place_ref[...], (((0,), (1,)), ((), ())), preferred_element_type=F32
            )
            for b in range(blocks):
                side[b, cols, :] = value[:, b * LANES : (b + 1) * LANES]

        loop(0, lanes // wide, unpack)

        def slot_step(s):
            g = h * chunk + s

            @pl.when(g + buffers - 1 < slots)
            def _():
                leg_copy(g + buffers - 1).start()

            mine = pl.ds(s, items, stride=chunk)
            upper = jnp.concatenate([side[b, mine, :] for b in range(half)], axis=1)
            lower = jnp.concatenate([side[b, mine, :] for b in range(half, blocks)], axis=1)
            both = jnp.concatenate([upper, lower], axis=0)[:, :north].astype(BF16)
            leg_copy(g).wait()
            table = leg_buf[lax.rem(g, buffers)]
            result = jnp.dot(both, table, preferred_element_type=F32)
            offsets = lax.broadcasted_iota(jnp.int32, (1, total), 1) - wave_ref[me * slots + g]
            sign = jnp.where(offsets % 2 == 0, 1.0, -1.0).astype(F32)
            spec = jnp.where(offsets >= 0, result[:items] + sign * result[items:], 0.0)

            @pl.when(g >= 2)
            def _():
                spec_copy(g - 2).wait()

            spec_buf[lax.rem(g, 2)] = spec.astype(BF16)
            spec_copy(g).start()
            filtered = (spec * spectrum_ref[...].reshape(1, total)).astype(BF16).astype(F32)
            second = jnp.concatenate([filtered, filtered * sign], axis=0).astype(BF16)
            folded = lax.dot_general(second, table, (((1,), (1,)), ((), ())), preferred_element_type=F32)
            folded = folded.astype(BF16).astype(F32)
            if half * LANES > north:
                pad = jnp.zeros((2 * items, half * LANES - north), F32)
                folded = jnp.concatenate([folded, pad], axis=1)
            for b in range(half):
                part = slice(b * LANES, (b + 1) * LANES)
                fold[b, mine, :] = folded[:items, part]
                fold[half + b, mine, :] = folded[items:, part]

        loop(0, chunk, slot_step)

        def pack(t):
            cols = pl.ds(pl.multiple_of(t * wide, wide), wide)
            value = jnp.concatenate([fold[b, cols, :] for b in range(blocks)], axis=1).astype(BF16)
            rows = lax.dot_general(
                place_ref[...], value, (((0,), (1,)), ((), ())), preferred_element_type=F32
            )
            back[h, :, :, cols] = rows.reshape(owners, rows_dev, wide).astype(BF16)

        loop(0, lanes // wide, pack)
        loop(1, owners, lambda i: out_back(h, far_first(i)).start())
        returned[h, me] = back[h, me]

    loop(0, chunks, middle_chunk)
    spec_copy(slots - 2).wait()
    spec_copy(slots - 1).wait()

    scale = 1.0 / math.sqrt(owners * slots)
    tiles = levels * rows_dev // tile

    def smooth_copy(t):
        rows = pl.ds(pl.multiple_of(t * tile, tile), tile)
        return pltpu.make_async_copy(x_ref.at[rows], smooth_hbm.at[rows], smooth_sem.at[t])

    def inverse_chunk(h):
        loop(1, owners, lambda d: in_back(h, d).wait_recv())
        for k in range(levels):
            parts = [
                returned[h, w, :, k * piece : (k + 1) * piece].astype(F32) for w in range(owners)
            ]
            y_ref[k * rows_dev : (k + 1) * rows_dev, :] = jnp.concatenate(parts, axis=1)

        def dot_step(t):
            rows = pl.ds(pl.multiple_of(t * tile, tile), tile)
            term = jnp.dot(y_ref[rows, :].astype(BF16), table_ref[h], preferred_element_type=F32)

            @pl.when(h == 0)
            def _():
                total_ref[rows, :] = term

            @pl.when(jnp.logical_and(h > 0, h < chunks - 1))
            def _():
                total_ref[rows, :] += term

            @pl.when(h == chunks - 1)
            def _():
                x_ref[rows, :] = ((total_ref[rows, :] + term) * scale).astype(BF16)
                smooth_copy(t).start()

        loop(0, tiles, dot_step)

    loop(0, chunks, inverse_chunk)

    def finish(h):
        loop(1, owners, lambda d: out_copy(h, d).wait_send())
        loop(1, owners, lambda d: out_back(h, d).wait_send())

    loop(0, chunks, finish)
    loop(0, tiles, lambda t: smooth_copy(t).wait())


def exchange(chunks, owners, rows_dev, waves, x, phases, picks, column, table, spectrum):
    slots, north, total = table.shape
    lon_cells = x.shape[1]
    levels = x.shape[0] // rows_dev
    chunk = slots // chunks
    lanes = 2 * levels * chunk
    columns = owners * 2 * chunk
    lat_rows = owners * rows_dev
    blocks = 2 * up(north, LANES) // LANES
    tiles = levels // 8
    hbm = pl.BlockSpec(memory_space=pl.ANY)
    vmem = pl.BlockSpec(memory_space=pltpu.VMEM)
    block = (chunks, owners, rows_dev, lanes)
    sems = pltpu.SemaphoreType.DMA
    return pl.pallas_call(
        functools.partial(exchange_body, owners, chunks),
        in_specs=[pl.BlockSpec(memory_space=pltpu.SMEM), hbm, hbm, vmem, vmem, hbm, vmem],
        out_specs=[hbm, hbm],
        out_shape=[
            jax.ShapeDtypeStruct((slots, 2 * levels, total), BF16),
            jax.ShapeDtypeStruct(x.shape, BF16),
        ],
        scratch_shapes=[
            pltpu.VMEM(x.shape, BF16),
            pltpu.VMEM(phases.shape, BF16),
            pltpu.VMEM((chunks, columns, lon_cells), BF16),
            pltpu.VMEM((x.shape[0], columns), F32),
            pltpu.VMEM(x.shape, F32),
            pltpu.VMEM((blocks * LANES, lat_rows), BF16),
            pltpu.VMEM(block, BF16),
            pltpu.VMEM(block, BF16),
            pltpu.VMEM(block, BF16),
            pltpu.VMEM(block, BF16),
            pltpu.VMEM((blocks, lanes, LANES), F32),
            pltpu.VMEM((blocks, lanes, LANES), F32),
            pltpu.VMEM((4, north, total), BF16),
            pltpu.VMEM((2, 2 * levels, total), BF16),
            sems((chunks, owners)),
            sems((chunks, owners)),
            sems((chunks, owners)),
            sems((chunks, owners)),
            sems((2,)),
            sems((4,)),
            sems((2,)),
            sems((tiles,)),
        ],
        compiler_params=params(collective_id=0, has_side_effects=True),
        cost_estimate=pl.CostEstimate(
            flops=2 * x.size * columns * chunks + 8 * slots * north * total * 2 * levels,
            bytes_accessed=2 * (x.size + table.size) + 8 * x.size,
            transcendentals=0,
        ),
        name="fourier_legendre_exchange",
    )(waves, x, phases, picks, column, table, spectrum)


def kernels_fit(owners, items, rows_dev, slots, north, total, lon_cells):
    chunk = slots // PARTS
    piece = 2 * chunk
    group = LANES // math.gcd(piece, LANES)
    return (
        slots % PARTS == 0
        and rows_dev % 8 == 0
        and items % 8 == 0
        and items % group == 0
        and total % LANES == 0
        and lon_cells % 512 == 0
        and owners * piece % 16 == 0
        and slots > 4
        and owners % 2 == 0
    )


def local_kernels(grid_grad, legendre, spectrum, owner_waves, lat_order):
    owners = lax.axis_size("wave")
    items, rows_dev, lon_cells = grid_grad.shape
    slots, total, north = legendre.shape
    waves = owner_waves.reshape(owners, slots)
    x = grid_grad.reshape(items * rows_dev, lon_cells)
    table = jnp.swapaxes(legendre, 1, 2)
    chunk = slots // PARTS
    in_chunks = jnp.swapaxes(waves.reshape(owners, PARTS, chunk), 0, 1)
    picks = jnp.stack([in_chunks, in_chunks + owners * slots], axis=2).reshape(PARTS, 1, -1)
    phases = jnp.asarray(phase_constants(owners * slots, lon_cells))
    spec, smoothed = exchange(
        PARTS, owners, rows_dev, owner_waves, x, phases, picks, lat_order, table, spectrum
    )
    return (spec, smoothed.reshape(grid_grad.shape))


def phase_table(waves, lon_cells, factor):
    ticks = lax.iota(jnp.int32, lon_cells)
    turns = waves[..., None] * ticks % lon_cells
    angle = turns.astype(jnp.float32) * (2.0 * math.pi / lon_cells)
    return jnp.stack([jnp.cos(angle), -jnp.sin(angle)], axis=1) * factor


def split_table(table):
    high_part = table.astype(jnp.bfloat16)
    low_part = (table - high_part.astype(jnp.float32)).astype(jnp.bfloat16)
    return (high_part, low_part)


def row_signs(count, wave):
    offsets = lax.iota(jnp.int32, count) - wave[..., None]
    return ((1 - 2 * (offsets % 2)).astype(jnp.float32), offsets >= 0)


def legendre_padded(legendre, side, spectrum, mine):
    half = side.shape[2] // 2
    result = jnp.einsum("snj,sjc->scn", legendre, side, preferred_element_type=jnp.float32)
    sign, valid = row_signs(legendre.shape[1], mine)
    spec = jnp.where(valid[:, None, :], result[:, :half] + sign[:, None, :] * result[:, half:], 0.0)
    filtered = (spec * spectrum).astype(jnp.bfloat16)
    second = jnp.concatenate([filtered, filtered * sign[:, None, :].astype(jnp.bfloat16)], axis=1)
    folded = jnp.einsum("snj,scn->scj", legendre, second, preferred_element_type=jnp.float32)
    return (spec, folded)


def local_plain(grid_grad, legendre, spectrum, owner_waves, lat_order):
    owners = lax.axis_size("wave")
    fields_levels, rows_dev, lon_cells = grid_grad.shape
    slots, total_rows, north_rows = legendre.shape
    lat_rows = rows_dev * owners
    waves = owner_waves.reshape(owners, slots)
    mine = lax.dynamic_index_in_dim(waves, lax.axis_index("wave"), 0, keepdims=False)
    forward_high, forward_low = split_table(
        phase_table(waves, lon_cells, 1.0 / math.sqrt(lon_cells))
    )
    inverse_high, inverse_low = split_table(
        phase_table(waves, lon_cells, 1.0 / math.sqrt(owners * slots))
    )
    onehot = (lat_order[None, :] == lax.iota(jnp.int32, lat_rows)[:, None]).astype(jnp.bfloat16)
    onehot = onehot.reshape(2, north_rows, owners, rows_dev)
    fourier = jnp.einsum(
        "kri,wpsi->wkrps", grid_grad, forward_high, preferred_element_type=jnp.float32
    )
    fourier = fourier + jnp.einsum(
        "kri,wpsi->wkrps", grid_grad, forward_low, preferred_element_type=jnp.float32
    )
    fourier = fourier.astype(jnp.bfloat16).reshape(owners, fields_levels, rows_dev, 2 * slots)
    received = lax.all_to_all(fourier, "wave", split_axis=0, concat_axis=0, tiled=True)
    items = received.shape[1]
    split = received.reshape(owners, items, rows_dev, 2, slots)
    side = jnp.einsum("hjwr,wkrps->sjhkp", onehot, split, preferred_element_type=jnp.float32)
    side = side.astype(jnp.bfloat16).reshape(slots, north_rows, 4 * items)
    spec, folded = legendre_padded(legendre, side, spectrum, mine)
    folded = folded.astype(jnp.bfloat16).reshape(slots, 2, items, 2, north_rows)
    back = jnp.einsum("hjwr,shkpj->wkrps", onehot, folded, preferred_element_type=jnp.float32)
    back = back.astype(jnp.bfloat16).reshape(owners, items, rows_dev, 2 * slots)
    returned = lax.all_to_all(back, "wave", split_axis=0, concat_axis=0, tiled=True)
    spec_out = spec.reshape(slots, items, 2, total_rows).astype(jnp.bfloat16)
    spec_out, returned = (spec_out, returned)
    gradient_spectra = spec_out.reshape(slots, 2 * fields_levels, total_rows)
    returned = returned.reshape(owners, fields_levels, rows_dev, 2, slots)
    smoothed = jnp.einsum(
        "wkrps,wpsi->kri", returned, inverse_high, preferred_element_type=jnp.float32
    )
    smoothed = smoothed + jnp.einsum(
        "wkrps,wpsi->kri", returned, inverse_low, preferred_element_type=jnp.float32
    )
    return (gradient_spectra, smoothed.astype(jnp.bfloat16))


def local(grid_grad, legendre, spectrum, owner_waves, lat_order):
    slots, total, north = legendre.shape
    if kernels_fit(lax.axis_size("wave"), *grid_grad.shape[:2], slots, north, total, grid_grad.shape[2]):
        return local_kernels(grid_grad, legendre, spectrum, owner_waves, lat_order)
    return local_plain(grid_grad, legendre, spectrum, owner_waves, lat_order)


def solution(mesh):
    in_specs = (P("members", "wave", None), P("wave", None, None), P(), P(), P())
    out_specs = (P(("members", "wave"), None, None), P("members", "wave", None))
    return jax.shard_map(local, mesh=mesh, in_specs=in_specs, out_specs=out_specs, check_vma=False)
```

```python
import functools
import math

import jax
import ml_dtypes
import numpy as np
import jax.numpy as jnp
from jax import lax
from jax.experimental import pallas as pl
from jax.experimental.pallas import tpu as pltpu
from jax.sharding import PartitionSpec as P

LANES = 128
PARTS = 4
VMEM = 62 * 2**20
F32 = jnp.float32
BF16 = jnp.bfloat16


def up(value, step):
    return -(-value // step) * step


def params(**extra):
    return pltpu.CompilerParams(vmem_limit_bytes=VMEM, **extra)


def phase_constants(count, lon_cells):
    turns = np.arange(count)[:, None] * np.arange(lon_cells)[None, :] % lon_cells
    angle = turns * (2.0 * np.pi / lon_cells)
    return np.concatenate([np.cos(angle), -np.sin(angle)], axis=0).astype(ml_dtypes.bfloat16)


def exchange_body(
    owners, chunks, wave_ref, x_hbm, phase_hbm, pick_ref, lat_ref, leg_hbm, spectrum_ref,
    spec_hbm, smooth_hbm,
    x_ref, phase_ref, table_ref, y_ref, total_ref, place_ref,
    sent, recv, back, returned, side, fold, leg_buf, spec_buf,
    fsend, frecv, bsend, brecv, load_sem, leg_sem, spec_sem, smooth_sem,
):
    slots, north, total = leg_hbm.shape
    lon_cells = x_hbm.shape[1]
    chunk = slots // chunks
    piece = 2 * chunk
    rows_dev = sent.shape[2]
    lanes = sent.shape[3]
    levels = lanes // piece
    items = lanes // chunk
    columns = owners * piece
    lat_rows = owners * rows_dev
    blocks = side.shape[0]
    half = blocks // 2
    buffers = leg_buf.shape[0]
    me = lax.axis_index("wave")

    load_x = pltpu.make_async_copy(x_hbm, x_ref, load_sem.at[0])
    load_phase = pltpu.make_async_copy(phase_hbm, phase_ref, load_sem.at[1])
    load_phase.start()
    load_x.start()

    def leg_copy(g):
        slot = lax.rem(g, buffers)
        return pltpu.make_async_copy(leg_hbm.at[g], leg_buf.at[slot], leg_sem.at[slot])

    def spec_copy(g):
        slot = lax.rem(g, 2)
        return pltpu.make_async_copy(spec_buf.at[slot], spec_hbm.at[g], spec_sem.at[slot])

    def out_copy(h, d):
        target = lax.rem(me + d, owners)
        return pltpu.make_async_remote_copy(
            src_ref=sent.at[h, target], dst_ref=recv.at[h, me],
            send_sem=fsend.at[h, d], recv_sem=frecv.at[h, d],
            device_id={"wave": target}, device_id_type=pl.DeviceIdType.MESH,
        )

    def in_copy(h, d):
        source = lax.rem(me + owners - d, owners)
        return pltpu.make_async_remote_copy(
            src_ref=sent.at[h, source], dst_ref=recv.at[h, source],
            send_sem=fsend.at[h, d], recv_sem=frecv.at[h, d],
            device_id={"wave": source}, device_id_type=pl.DeviceIdType.MESH,
        )

    def out_back(h, d):
        target = lax.rem(me + d, owners)
        return pltpu.make_async_remote_copy(
            src_ref=back.at[h, target], dst_ref=returned.at[h, me],
            send_sem=bsend.at[h, d], recv_sem=brecv.at[h, d],
            device_id={"wave": target}, device_id_type=pl.DeviceIdType.MESH,
        )

    def in_back(h, d):
        source = lax.rem(me + owners - d, owners)
        return pltpu.make_async_remote_copy(
            src_ref=back.at[h, source], dst_ref=returned.at[h, source],
            send_sem=bsend.at[h, d], recv_sem=brecv.at[h, d],
            device_id={"wave": source}, device_id_type=pl.DeviceIdType.MESH,
        )

    def loop(low, high, step):
        def body(i, carry):
            step(i)
            return carry

        lax.fori_loop(low, high, body, 0)

    barrier = pltpu.get_barrier_semaphore()

    def greet(d):
        pl.semaphore_signal(
            barrier, inc=1, device_id={"wave": lax.rem(me + d, owners)}, device_id_type=pl.DeviceIdType.MESH
        )

    loop(1, owners, greet)
    lat = lat_ref[...].reshape(1, lat_rows)
    column = jnp.where(lat < north, lat, lat - north + half * LANES)
    place_ref[...] = jnp.where(
        lax.broadcasted_iota(jnp.int32, place_ref.shape, 0) == column, 1.0, 0.0
    ).astype(BF16)
    load_phase.wait()

    def table_chunk(h):
        rows = lax.broadcasted_iota(jnp.int32, (phase_ref.shape[0], columns), 0)
        pick = jnp.where(rows == pick_ref[h], 1.0, 0.0).astype(BF16)

        def lon_step(t):
            cells = pl.ds(pl.multiple_of(t * 512, 512), 512)
            table_ref[h, :, cells] = lax.dot_general(
                pick, phase_ref[:, cells], (((0,), (0,)), ((), ())), preferred_element_type=F32
            ).astype(BF16)

        loop(0, lon_cells // 512, lon_step)

    factor = 1.0 / math.sqrt(lon_cells)
    tile = 4 * rows_dev * 2

    def forward_chunk(h):
        table_chunk(h)

        @pl.when(h == 0)
        def _():
            load_x.wait()

        def dot_step(t):
            rows = pl.ds(pl.multiple_of(t * tile, tile), tile)
            y_ref[rows, :] = lax.dot_general(
                x_ref[rows, :], table_ref[h], (((1,), (1,)), ((), ())), preferred_element_type=F32
            ) * factor

        loop(0, levels * rows_dev // tile, dot_step)
        for w in range(owners):
            parts = [
                y_ref[k * rows_dev : (k + 1) * rows_dev, w * piece : (w + 1) * piece] for k in range(levels)
            ]
            sent[h, w] = jnp.concatenate(parts, axis=1).astype(BF16)

        @pl.when(h == 0)
        def _():
            pl.semaphore_wait(barrier, owners - 1)

        loop(1, owners, lambda d: out_copy(h, d).start())
        recv[h, me] = sent[h, me]

    loop(0, chunks, forward_chunk)
    for g in range(buffers - 1):
        leg_copy(g).start()

    wide = 128

    def middle_chunk(h):
        loop(1, owners, lambda d: in_copy(h, d).wait_recv())

        def unpack(t):
            cols = pl.ds(pl.multiple_of(t * wide, wide), wide)
            rows = recv[h, :, :, cols].astype(F32).reshape(lat_rows, wide).astype(BF16)
            value = lax.dot_general(
                rows, place_ref[...], (((0,), (1,)), ((), ())), preferred_element_type=F32
            )
            for b in range(blocks):
                side[b, cols, :] = value[:, b * LANES : (b + 1) * LANES]

        loop(0, lanes // wide, unpack)

        def slot_step(s):
            g = h * chunk + s

            @pl.when(g + buffers - 1 < slots)
            def _():
                leg_copy(g + buffers - 1).start()

            mine = pl.ds(s, items, stride=chunk)
            upper = jnp.concatenate([side[b, mine, :] for b in range(half)], axis=1)
            lower = jnp.concatenate([side[b, mine, :] for b in range(half, blocks)], axis=1)
            both = jnp.concatenate([upper, lower], axis=0)[:, :north].astype(BF16)
            leg_copy(g).wait()
            table = leg_buf[lax.rem(g, buffers)]
            result = jnp.dot(both, table, preferred_element_type=F32)
            offsets = lax.broadcasted_iota(jnp.int32, (1, total), 1) - wave_ref[me * slots + g]
            sign = jnp.where(offsets % 2 == 0, 1.0, -1.0).astype(F32)
            spec = jnp.where(offsets >= 0, result[:items] + sign * result[items:], 0.0)

            @pl.when(g >= 2)
            def _():
                spec_copy(g - 2).wait()

            spec_buf[lax.rem(g, 2)] = spec.astype(BF16)
            spec_copy(g).start()
            filtered = (spec * spectrum_ref[...].reshape(1, total)).astype(BF16).astype(F32)
            second = jnp.concatenate([filtered, filtered * sign], axis=0).astype(BF16)
            folded = lax.dot_general(second, table, (((1,), (1,)), ((), ())), preferred_element_type=F32)
            folded = folded.astype(BF16).astype(F32)
            if half * LANES > north:
                pad = jnp.zeros((2 * items, half * LANES - north), F32)
                folded = jnp.concatenate([folded, pad], axis=1)
            for b in range(half):
                part = slice(b * LANES, (b + 1) * LANES)
                fold[b, mine, :] = folded[:items, part]
                fold[half + b, mine, :] = folded[items:, part]

        loop(0, chunk, slot_step)

        def pack(t):
            cols = pl.ds(pl.multiple_of(t * wide, wide), wide)
            value = jnp.concatenate([fold[b, cols, :] for b in range(blocks)], axis=1).astype(BF16)
            rows = lax.dot_general(
                place_ref[...], value, (((0,), (1,)), ((), ())), preferred_element_type=F32
            )
            back[h, :, :, cols] = rows.reshape(owners, rows_dev, wide).astype(BF16)

        loop(0, lanes // wide, pack)
        loop(1, owners, lambda d: out_back(h, d).start())
        returned[h, me] = back[h, me]

    loop(0, chunks, middle_chunk)
    spec_copy(slots - 2).wait()
    spec_copy(slots - 1).wait()

    scale = 1.0 / math.sqrt(owners * slots)
    tiles = levels * rows_dev // tile

    def smooth_copy(t):
        rows = pl.ds(pl.multiple_of(t * tile, tile), tile)
        return pltpu.make_async_copy(x_ref.at[rows], smooth_hbm.at[rows], smooth_sem.at[t])

    def inverse_chunk(h):
        loop(1, owners, lambda d: in_back(h, d).wait_recv())
        for k in range(levels):
            parts = [
                returned[h, w, :, k * piece : (k + 1) * piece].astype(F32) for w in range(owners)
            ]
            y_ref[k * rows_dev : (k + 1) * rows_dev, :] = jnp.concatenate(parts, axis=1)

        def dot_step(t):
            rows = pl.ds(pl.multiple_of(t * tile, tile), tile)
            term = jnp.dot(y_ref[rows, :].astype(BF16), table_ref[h], preferred_element_type=F32)

            @pl.when(h == 0)
            def _():
                total_ref[rows, :] = term

            @pl.when(jnp.logical_and(h > 0, h < chunks - 1))
            def _():
                total_ref[rows, :] += term

            @pl.when(h == chunks - 1)
            def _():
                x_ref[rows, :] = ((total_ref[rows, :] + term) * scale).astype(BF16)
                smooth_copy(t).start()

        loop(0, tiles, dot_step)

    loop(0, chunks, inverse_chunk)

    def finish(h):
        loop(1, owners, lambda d: out_copy(h, d).wait_send())
        loop(1, owners, lambda d: out_back(h, d).wait_send())

    loop(0, chunks, finish)
    loop(0, tiles, lambda t: smooth_copy(t).wait())


def exchange(chunks, owners, rows_dev, waves, x, phases, picks, column, table, spectrum):
    slots, north, total = table.shape
    lon_cells = x.shape[1]
    levels = x.shape[0] // rows_dev
    chunk = slots // chunks
    lanes = 2 * levels * chunk
    columns = owners * 2 * chunk
    lat_rows = owners * rows_dev
    blocks = 2 * up(north, LANES) // LANES
    tiles = levels // 8
    hbm = pl.BlockSpec(memory_space=pl.ANY)
    vmem = pl.BlockSpec(memory_space=pltpu.VMEM)
    block = (chunks, owners, rows_dev, lanes)
    sems = pltpu.SemaphoreType.DMA
    return pl.pallas_call(
        functools.partial(exchange_body, owners, chunks),
        in_specs=[pl.BlockSpec(memory_space=pltpu.SMEM), hbm, hbm, vmem, vmem, hbm, vmem],
        out_specs=[hbm, hbm],
        out_shape=[
            jax.ShapeDtypeStruct((slots, 2 * levels, total), BF16),
            jax.ShapeDtypeStruct(x.shape, BF16),
        ],
        scratch_shapes=[
            pltpu.VMEM(x.shape, BF16),
            pltpu.VMEM(phases.shape, BF16),
            pltpu.VMEM((chunks, columns, lon_cells), BF16),
            pltpu.VMEM((x.shape[0], columns), F32),
            pltpu.VMEM(x.shape, F32),
            pltpu.VMEM((blocks * LANES, lat_rows), BF16),
            pltpu.VMEM(block, BF16),
            pltpu.VMEM(block, BF16),
            pltpu.VMEM(block, BF16),
            pltpu.VMEM(block, BF16),
            pltpu.VMEM((blocks, lanes, LANES), F32),
            pltpu.VMEM((blocks, lanes, LANES), F32),
            pltpu.VMEM((4, north, total), BF16),
            pltpu.VMEM((2, 2 * levels, total), BF16),
            sems((chunks, owners)),
            sems((chunks, owners)),
            sems((chunks, owners)),
            sems((chunks, owners)),
            sems((2,)),
            sems((4,)),
            sems((2,)),
            sems((tiles,)),
        ],
        compiler_params=params(collective_id=0, has_side_effects=True),
        cost_estimate=pl.CostEstimate(
            flops=2 * x.size * columns * chunks + 8 * slots * north * total * 2 * levels,
            bytes_accessed=2 * (x.size + table.size) + 8 * x.size,
            transcendentals=0,
        ),
        name="fourier_legendre_exchange",
    )(waves, x, phases, picks, column, table, spectrum)


def kernels_fit(owners, items, rows_dev, slots, north, total, lon_cells):
    chunk = slots // PARTS
    piece = 2 * chunk
    group = LANES // math.gcd(piece, LANES)
    return (
        slots % PARTS == 0
        and rows_dev % 8 == 0
        and items % 8 == 0
        and items % group == 0
        and total % LANES == 0
        and lon_cells % 512 == 0
        and owners * piece % 16 == 0
        and slots > 4
    )


def local_kernels(grid_grad, legendre, spectrum, owner_waves, lat_order):
    owners = lax.axis_size("wave")
    items, rows_dev, lon_cells = grid_grad.shape
    slots, total, north = legendre.shape
    waves = owner_waves.reshape(owners, slots)
    x = grid_grad.reshape(items * rows_dev, lon_cells)
    table = jnp.swapaxes(legendre, 1, 2)
    chunk = slots // PARTS
    in_chunks = jnp.swapaxes(waves.reshape(owners, PARTS, chunk), 0, 1)
    picks = jnp.stack([in_chunks, in_chunks + owners * slots], axis=2).reshape(PARTS, 1, -1)
    phases = jnp.asarray(phase_constants(owners * slots, lon_cells))
    spec, smoothed = exchange(
        PARTS, owners, rows_dev, owner_waves, x, phases, picks, lat_order, table, spectrum
    )
    return (spec, smoothed.reshape(grid_grad.shape))


def phase_table(waves, lon_cells, factor):
    ticks = lax.iota(jnp.int32, lon_cells)
    turns = waves[..., None] * ticks % lon_cells
    angle = turns.astype(jnp.float32) * (2.0 * math.pi / lon_cells)
    return jnp.stack([jnp.cos(angle), -jnp.sin(angle)], axis=1) * factor


def split_table(table):
    high_part = table.astype(jnp.bfloat16)
    low_part = (table - high_part.astype(jnp.float32)).astype(jnp.bfloat16)
    return (high_part, low_part)


def row_signs(count, wave):
    offsets = lax.iota(jnp.int32, count) - wave[..., None]
    return ((1 - 2 * (offsets % 2)).astype(jnp.float32), offsets >= 0)


def legendre_padded(legendre, side, spectrum, mine):
    half = side.shape[2] // 2
    result = jnp.einsum("snj,sjc->scn", legendre, side, preferred_element_type=jnp.float32)
    sign, valid = row_signs(legendre.shape[1], mine)
    spec = jnp.where(valid[:, None, :], result[:, :half] + sign[:, None, :] * result[:, half:], 0.0)
    filtered = (spec * spectrum).astype(jnp.bfloat16)
    second = jnp.concatenate([filtered, filtered * sign[:, None, :].astype(jnp.bfloat16)], axis=1)
    folded = jnp.einsum("snj,scn->scj", legendre, second, preferred_element_type=jnp.float32)
    return (spec, folded)


def local_plain(grid_grad, legendre, spectrum, owner_waves, lat_order):
    owners = lax.axis_size("wave")
    fields_levels, rows_dev, lon_cells = grid_grad.shape
    slots, total_rows, north_rows = legendre.shape
    lat_rows = rows_dev * owners
    waves = owner_waves.reshape(owners, slots)
    mine = lax.dynamic_index_in_dim(waves, lax.axis_index("wave"), 0, keepdims=False)
    forward_high, forward_low = split_table(
        phase_table(waves, lon_cells, 1.0 / math.sqrt(lon_cells))
    )
    inverse_high, inverse_low = split_table(
        phase_table(waves, lon_cells, 1.0 / math.sqrt(owners * slots))
    )
    onehot = (lat_order[None, :] == lax.iota(jnp.int32, lat_rows)[:, None]).astype(jnp.bfloat16)
    onehot = onehot.reshape(2, north_rows, owners, rows_dev)
    fourier = jnp.einsum(
        "kri,wpsi->wkrps", grid_grad, forward_high, preferred_element_type=jnp.float32
    )
    fourier = fourier + jnp.einsum(
        "kri,wpsi->wkrps", grid_grad, forward_low, preferred_element_type=jnp.float32
    )
    fourier = fourier.astype(jnp.bfloat16).reshape(owners, fields_levels, rows_dev, 2 * slots)
    received = lax.all_to_all(fourier, "wave", split_axis=0, concat_axis=0, tiled=True)
    items = received.shape[1]
    split = received.reshape(owners, items, rows_dev, 2, slots)
    side = jnp.einsum("hjwr,wkrps->sjhkp", onehot, split, preferred_element_type=jnp.float32)
    side = side.astype(jnp.bfloat16).reshape(slots, north_rows, 4 * items)
    spec, folded = legendre_padded(legendre, side, spectrum, mine)
    folded = folded.astype(jnp.bfloat16).reshape(slots, 2, items, 2, north_rows)
    back = jnp.einsum("hjwr,shkpj->wkrps", onehot, folded, preferred_element_type=jnp.float32)
    back = back.astype(jnp.bfloat16).reshape(owners, items, rows_dev, 2 * slots)
    returned = lax.all_to_all(back, "wave", split_axis=0, concat_axis=0, tiled=True)
    spec_out = spec.reshape(slots, items, 2, total_rows).astype(jnp.bfloat16)
    spec_out, returned = (spec_out, returned)
    gradient_spectra = spec_out.reshape(slots, 2 * fields_levels, total_rows)
    returned = returned.reshape(owners, fields_levels, rows_dev, 2, slots)
    smoothed = jnp.einsum(
        "wkrps,wpsi->kri", returned, inverse_high, preferred_element_type=jnp.float32
    )
    smoothed = smoothed + jnp.einsum(
        "wkrps,wpsi->kri", returned, inverse_low, preferred_element_type=jnp.float32
    )
    return (gradient_spectra, smoothed.astype(jnp.bfloat16))


def local(grid_grad, legendre, spectrum, owner_waves, lat_order):
    slots, total, north = legendre.shape
    if kernels_fit(lax.axis_size("wave"), *grid_grad.shape[:2], slots, north, total, grid_grad.shape[2]):
        return local_kernels(grid_grad, legendre, spectrum, owner_waves, lat_order)
    return local_plain(grid_grad, legendre, spectrum, owner_waves, lat_order)


def solution(mesh):
    in_specs = (P("members", "wave", None), P("wave", None, None), P(), P(), P())
    out_specs = (P(("members", "wave"), None, None), P("members", "wave", None))
    return jax.shard_map(local, mesh=mesh, in_specs=in_specs, out_specs=out_specs, check_vma=False)
```
